512 devices in a mesh: slab: 64 (over y, z), pencil: 8 (over x, core).
Axes of the slice: x: 4, y: 4, z: 16, core: 2. Of those that a mesh axis runs over, the one named last changes fastest.
Arguments:
- coefficients: bfloat16 [32768, 128], P(('slab', 'pencil')), may hold values from -6 to 6
- projection: bfloat16 [32768, 64, 128], P(('slab', 'pencil')), may hold values from -0.5 to 0.5
- near_blocks: bfloat16 [32768, 1, 128, 128], P(('slab', 'pencil')), may hold values from -0.5 to 0.5
- near_ids: int32 [32768, 1], P(('slab', 'pencil')), may hold values from 0 to 32767, as said below
- grid_slab: int32 [32768, 1], P(('slab', 'pencil')), may hold values from 0 to 63; in each aligned block of 64 rows (0 to 63, 64 to 127, ...) at most 2 rows name the same one
- anchors: int32 [3, 32768], P(None, ('slab', 'pencil')), may hold values from 0 to 124, as said below
- spectrum: float32 [512, 128, 1024], P('pencil', 'slab'), may hold values from 0.3 to 13500, as said below
Outputs:
- fields: float32 [32768, 128], P(('slab', 'pencil'))
The draws below stay inside these ranges and needn't reach their ends.
Inputs may be any that keep to these rules, and one draw needn't show every extreme that they name: `grid_slab`: among the rows of one device at most 2 boxes name the same slab; in every draw some device names one slab exactly 2 times. `anchors`: row 0 lies in 0 to 4, row 1 in 0 to 124, row 2 in 0 to 124, so a stencil stays inside one device's block of the grid; each bound is reached. `near_ids`: box b's near ids name boxes of its own slab group, from 512 * (b // 512) to 512 * (b // 512) + 511. `spectrum`: the kernel is real and even: kernel at frequency (kx, kz, ky) equals kernel at ((512 - kx) % 512, (128 - kz) % 128, (1024 - ky) % 1024).
All inputs are finite; a program needn't handle non-finite values.
Results may differ from the reference program's by a relative error of at most 0.006.
Values may be sent and summed in bfloat16 or wider, within the bound.
No kernel may reach another device: no remote copies, remote signals or barrier semaphores. Data moves between devices by JAX's collectives and lax.ppermute only.
A program may use at most 64 MiB of HBM per device.

```python
import math
import jax
import jax.numpy as jnp
import numpy as np
from jax import lax

FUNCS = 128
STENCIL = 64
NEAR = 1
BOX_DEV = 64
CX = 8
CY = 128
NZ = 128
NX = 512
NY = 1024
GROUP_BOXES = 512
BOXES = 32768
CAP = 2
N_SLAB = 64
N_PENCIL = 8


def draw_anchors(key, part):
    key = jax.random.fold_in(key, 7)
    keys = jax.random.split(key, 3)
    along_x = jax.random.randint(keys[0], (BOXES,), 0, CX - 3)
    along_y = jax.random.randint(keys[1], (BOXES,), 0, CY - 3)
    along_z = jax.random.randint(keys[2], (BOXES,), 0, NZ - 3)
    along_x = along_x.at[0].set(CX - 4)
    along_y = along_y.at[0].set(CY - 4)
    along_z = along_z.at[0].set(NZ - 4)
    return jnp.stack([along_x, along_y, along_z]).astype(jnp.int32)


def draw_near_ids(key, part):
    key = jax.random.fold_in(key, 9)
    offset = jax.random.randint(key, (BOXES, NEAR), 0, GROUP_BOXES)
    first = jnp.arange(BOXES, dtype=jnp.int32) // GROUP_BOXES * GROUP_BOXES
    chosen = first[:, None] + offset
    chosen = chosen.at[0, 0].set(0)
    chosen = chosen.at[BOXES - 1, 0].set(BOXES - 1)
    return chosen.astype(jnp.int32)


def mirror_axis(values, axis):
    return jnp.roll(jnp.flip(values, axis), 1, axis)


def draw_spectrum(key, part):
    key = jax.random.fold_in(key, 11)
    slots = jnp.arange(NZ, dtype=jnp.int32)
    pair = slots // 2
    frequency_z = jnp.where(slots % 2 == 0, pair, jnp.where(pair == 0, NZ // 2, NZ - pair))
    frequency_x = jnp.arange(NX, dtype=jnp.int32)
    frequency_y = jnp.arange(NY, dtype=jnp.int32)
    sine_x = jnp.sin(math.pi * frequency_x.astype(jnp.float32) / NX)
    sine_z = jnp.sin(math.pi * frequency_z.astype(jnp.float32) / NZ)
    sine_y = jnp.sin(math.pi * frequency_y.astype(jnp.float32) / NY)
    laplace = 4.0 * (sine_x[:, None, None] ** 2 + sine_z[None, :, None] ** 2 + sine_y[None, None, :] ** 2)
    green = 8.0 / (0.0009 + laplace)
    raw = jax.random.uniform(key, (NX, NZ, NY), jnp.float32, -1.0, 1.0)
    partner_slot = jnp.where(slots < 2, slots, jnp.bitwise_xor(slots, 1))
    mirrored = mirror_axis(mirror_axis(jnp.take(raw, partner_slot, axis=1), 0), 2)
    factor = 1.0 + 0.4 * 0.5 * (raw + mirrored)
    return (green * factor).astype(jnp.float32)


def levels(rng, extent, pieces, low, largest):
    def one(axis_at, blocks):
        heights = jax.random.uniform(jax.random.fold_in(jax.random.fold_in(rng, 6), axis_at), (blocks,), jnp.float32, low / len(pieces), largest / len(pieces))
        return jnp.repeat(jnp.exp(heights), extent[axis_at] // blocks).reshape((-1,) + (1,) * (len(extent) - axis_at - 1))

    level = one(*pieces[0])
    for cut in pieces[1:]:
        level = level * one(*cut)
    return level


def assign_block(rng, own, number, rows, amount, top, most, slope):
    sequence = jax.random.permutation(rng, amount)
    packed, ordinary = load_shares(amount, rows * top, most, slope, True), load_shares(amount, rows * top, most, slope, False)
    places = jnp.arange(amount)

    def named(sizes, rotation):
        used = int((sizes > 0).sum())
        fixed = max(1, used // 4)
        shifted = fixed + (places - fixed + rotation * (used - fixed)) % max(1, amount - fixed)
        return jnp.zeros((amount,), jnp.int32).at[sequence[jnp.where(places < fixed, places, shifted)]].set(jnp.asarray(sizes, jnp.int32))

    sizes = jnp.where(number % 4 == 0, named(packed, number // 4), named(ordinary, number - number // 4 - 1))
    mixed = jax.random.permutation(jax.random.fold_in(own, 3), amount)
    donor, receiver = mixed[0:amount // 2 * 2:2], mixed[1:amount // 2 * 2:2]
    margin = jnp.minimum(sizes[donor] - 1, most - sizes[receiver]) // 2
    margin = jnp.where((donor == sequence[0]) | (receiver == sequence[0]) | (sizes[receiver] == 0), 0, jnp.maximum(margin, 0))
    shifted = jax.random.randint(jax.random.fold_in(own, 4), (amount // 2,), 0, 1 << 20) % (margin + 1)
    sizes = sizes.at[donor].add(-shifted).at[receiver].add(shifted)
    items = jnp.searchsorted(jnp.cumsum(sizes), jnp.arange(rows * top), side="right").astype(jnp.int32)
    listing = items.reshape(top, rows).T
    listing = listing[jax.random.permutation(jax.random.fold_in(own, 1), rows)]
    rotation = jax.random.randint(jax.random.fold_in(own, 2), (rows, 1), 0, top)
    return jnp.take_along_axis(listing, (jnp.arange(top)[None, :] + rotation) % top, axis=1)


def load_shares(number_of, total, reach, slope, full):
    weights = [(1 << 20) // math.isqrt(rank ** slope) + 1 for rank in range(1, number_of + 1)]
    largest = reach if full else min(reach, max(-(-total // number_of), total * weights[0] // sum(weights)))
    least = 1 if total - largest >= number_of - 1 else 0
    counts, surplus = [largest] + [least] * (number_of - 1), total - largest - least * (number_of - 1)
    while surplus > 0:
        candidates = [i for i in range(1, number_of) if counts[i] < largest] or [i for i in range(1, number_of) if counts[i] < reach]
        mass, left = sum([weights[i] for i in candidates]), surplus
        for i in candidates:
            extra = min(reach - counts[i], max(1, left * weights[i] // mass), surplus)
            counts[i] = counts[i] + extra
            surplus = surplus - extra
    return np.array(counts)


def normal_values(rng, shape, scale, bound, shards=(), kind=jnp.bfloat16):
    array = jax.random.normal(rng, shape, jnp.float32) * scale
    if len(shards) > 0:
        array = levels(rng, shape, shards, -0.22, 0.18) * array
    return jnp.clip(array, min=-bound, max=bound).astype(kind)


def setup_inputs(seed: int = 0) -> dict:
    arg_keys = jax.random.split(jax.random.key(seed), 8)
    coefficients = normal_values(arg_keys[0], (BOXES, FUNCS), 1.0, 6.0, ((0, 512),))
    projection = normal_values(arg_keys[1], (BOXES, STENCIL, FUNCS), FUNCS ** -0.5, 0.5, ((0, 512),))
    near_blocks = normal_values(arg_keys[2], (BOXES, NEAR, FUNCS, FUNCS), FUNCS ** -0.5, 0.5, ((0, 512),))
    near_ids = draw_near_ids(jax.random.fold_in(arg_keys[7], 71), 0)
    grid_slab_keys = jax.random.split(jax.random.fold_in(arg_keys[4], 1), BOXES // BOX_DEV)
    grid_slab_turns = jax.random.permutation(jax.random.fold_in(arg_keys[4], 3), BOXES // BOX_DEV)
    grid_slab = jax.vmap(lambda own, number: assign_block(jax.random.fold_in(arg_keys[4], 2), own, number, BOX_DEV, N_SLAB, 1, CAP, 2))(grid_slab_keys, grid_slab_turns).reshape((BOXES, 1))
    anchors = draw_anchors(jax.random.fold_in(arg_keys[7], 71), 0)
    spectrum = draw_spectrum(jax.random.fold_in(arg_keys[7], 71), 0)
    return {"coefficients": coefficients, "projection": projection, "near_blocks": near_blocks, "near_ids": near_ids, "grid_slab": grid_slab, "anchors": anchors, "spectrum": spectrum}


def box_cells(grid_slab, anchors):
    boxes = jnp.arange(BOXES, dtype=jnp.int32)
    pencil_of = (boxes // BOX_DEV) % N_PENCIL
    node = jnp.arange(STENCIL, dtype=jnp.int32)
    step_x = node // 16
    step_y = (node // 4) % 4
    step_z = node % 4
    cell_x = CX * grid_slab[:, 0][:, None] + anchors[0][:, None] + step_x[None, :]
    cell_y = CY * pencil_of[:, None] + anchors[1][:, None] + step_y[None, :]
    cell_z = anchors[2][:, None] + step_z[None, :]
    return cell_x.astype(jnp.int32), cell_z.astype(jnp.int32), cell_y.astype(jnp.int32)


def slot_of_frequency():
    freq = jnp.arange(NZ, dtype=jnp.int32)
    half = NZ // 2
    slot = jnp.where(freq == 0, 0, jnp.where(freq == half, 1, jnp.where(freq < half, 2 * freq, 2 * (NZ - freq) + 1)))
    return slot.astype(jnp.int32)


def reference(coefficients, projection, near_blocks, near_ids, grid_slab, anchors, spectrum):
    cell_x, cell_z, cell_y = box_cells(grid_slab, anchors)
    groups = (N_SLAB, GROUP_BOXES)

    def project(items):
        blocks, values = items
        return jnp.einsum("bnf,bf->bn", blocks.astype(jnp.float32), values.astype(jnp.float32))

    projected = lax.map(project, (projection.reshape(groups + (STENCIL, FUNCS)), coefficients.reshape(groups + (FUNCS,))))
    projected = projected.reshape(BOXES, STENCIL)
    grid = jnp.zeros((NX, NZ, NY), jnp.float32).at[cell_x, cell_z, cell_y].add(projected)
    kernel = jnp.take(spectrum, slot_of_frequency(), axis=1)
    potential = jnp.fft.ifftn(jnp.fft.fftn(grid) * kernel).real.astype(jnp.float32)
    sampled = potential[cell_x, cell_z, cell_y].astype(jnp.bfloat16)
    partner = coefficients[near_ids]

    def finish(items):
        blocks, samples, nears, others = items
        interp = jnp.einsum("bnf,bn->bf", blocks.astype(jnp.float32), samples.astype(jnp.float32))
        close = jnp.einsum("bmgf,bmf->bg", nears.astype(jnp.float32), others.astype(jnp.float32))
        return interp + close

    fields = lax.map(finish, (projection.reshape(groups + (STENCIL, FUNCS)), sampled.reshape(groups + (STENCIL,)),
                              near_blocks.reshape(groups + (NEAR, FUNCS, FUNCS)), partner.reshape(groups + (NEAR, FUNCS))))
    return fields.reshape(BOXES, FUNCS)
```

```python
import math

import jax
import jax.numpy as jnp
import numpy as np
from jax import lax
from jax.experimental import pallas as pl
from jax.experimental.pallas import tpu as pltpu
from jax.sharding import PartitionSpec as P

SLABS = 64
PENCILS = 8
BOX = 64
FUNCS = 128
STENCIL = 64
CX = 8
CY = 128
NX = 512
NY = 1024
NZ = 128
GROUP = BOX * PENCILS
ROWS = 24
LINES = NX // PENCILS
MORE = LINES + 8
BOXES = SLABS * BOX
TILE = 256

F32 = jnp.float32
BF16 = jnp.bfloat16
NT = (((1,), (1,)), ((), ()))
NN = (((1,), (0,)), ((), ()))


def halves(table):
    table = np.asarray(table, np.float32)
    high = table.astype(BF16)
    low = (table - high.astype(np.float32)).astype(BF16)
    return high, low


def x_table():
    phase = np.outer(np.arange(NX), np.arange(NX)) % NX * (2.0 * math.pi / NX)
    return np.concatenate([np.cos(phase), np.sin(phase)], 0)


def y_tables():
    phase = np.outer(np.arange(CY), np.arange(CY)) % CY * (2.0 * math.pi / CY)
    c, s = np.cos(phase), np.sin(phase)
    forward = np.block([[c, -s], [s, c]])
    inverse = np.block([[c, s], [-s, c]])
    turn = np.outer(np.arange(PENCILS), np.arange(CY)) * (2.0 * math.pi / NY)
    turn = np.concatenate([np.cos(turn), np.sin(turn)], 0).astype(np.float32)
    return forward, inverse, turn


def cosine_coefficients():
    fit = np.polynomial.chebyshev.Chebyshev.interpolate(
        lambda w: np.cos(2.0 * math.pi * np.sqrt(w)), 9, domain=[0.0, 0.25]
    )
    return [float(v) for v in fit.convert(kind=np.polynomial.Polynomial).coef]


COSINE = cosine_coefficients()


def cosine_of(step):
    u = (step.astype(F32) - (NZ // 2)) * (1.0 / NZ)
    w = u * u
    total = jnp.full_like(w, COSINE[-1])
    for value in COSINE[-2::-1]:
        total = total * w + value
    return -total


def iota(shape, axis):
    return lax.broadcasted_iota(jnp.int32, shape, axis)


def dot(a, b, dims=NN):
    return lax.dot_general(a, b, dims, preferred_element_type=F32)


def split(value):
    high = value.astype(BF16)
    return high, (value - high.astype(F32)).astype(BF16)


def project_kernel(meta_ref, coef_ref, proj_ref, send_ref, phase_ref, value_ref):
    coef = coef_ref[...]
    twice = jnp.concatenate([coef, coef], 0)
    lane = iota((STENCIL, 128), 1) & (BOX - 1)
    total = jnp.zeros((STENCIL, 128), F32)
    per = TILE // STENCIL
    for block in range(BOX // per):
        part = dot(proj_ref[block * TILE : (block + 1) * TILE, :], twice, NT)
        for t in range(per):
            total = jnp.where(
                lane == block * per + t, part[t * STENCIL : (t + 1) * STENCIL], total
            )
    value_ref[...] = total

    depth = meta_ref[0:1, :]
    second = (iota((SLABS, 128), 1) >= BOX).astype(jnp.int32)
    wave = iota((SLABS, 128), 0)
    for k in range(4):
        z = depth + k
        step = jnp.where(wave == 0, second * (NZ // 2) * z, wave * z + second * (NZ // 4))
        phase_ref[k] = cosine_of(step & (NZ - 1))

    turn = meta_ref[1:2, :] & 3
    row = iota((16, 128), 0) & 3
    parts = []
    for k in range(4):
        value = value_ref[pl.ds(k, 16, stride=4), :]
        out = value
        for m in range(1, 4):
            moved = jnp.where(row >= m, pltpu.roll(value, m, 0), pltpu.roll(value, m + 12, 0))
            out = jnp.where(turn == m, moved, out)
        parts.append(out)
    places = meta_ref[8:16, :].astype(F32)
    places = jnp.where(iota((8, 128), 1) < BOX, places * (1.0 / CX) - (SLABS // 2), places)
    for wave in range(SLABS):
        total = phase_ref[0, wave : wave + 1, :] * parts[0]
        for k in range(1, 4):
            total = total + phase_ref[k, wave : wave + 1, :] * parts[k]
        send_ref[wave] = jnp.concatenate([total, places], 0).astype(BF16)


def spread_kernel(place_ref, recv_ref, high_ref, low_ref, send_ref, pos_ref, row_ref, hot_ref):
    left = iota((ROWS, 128), 1) < BOX
    x_cells = iota((NX, 128), 0).astype(F32)
    y_cells = (iota((16, 8, 128), 0) * 8 + iota((16, 8, 128), 1)).astype(F32)
    upper = iota((8, 128), 0) < 4

    def fill(step, carry):
        for near in range(2):
            pair = step * 2 + near
            first = recv_ref[pair * 2].astype(F32)
            other = recv_ref[pair * 2 + 1].astype(F32)
            real = jnp.where(left, first, pltpu.roll(other, BOX, 1))
            imag = jnp.where(left, pltpu.roll(first, BOX, 1), other)
            x_place = (real[16:17] + (SLABS // 2)) * CX
            y_place = imag[16:17]
            pos_ref[pair] = jnp.concatenate(
                [x_place, y_place, jnp.zeros((6, 128), F32)], 0
            )
            start = pl.multiple_of(pair * 128, 128)
            away = y_cells - y_place[None]
            inside = (away >= 0.0) & (away < 4.0)
            for i in range(4):
                for c, source in enumerate((real, imag)):
                    block = source[8 * (i // 2) : 8 * (i // 2) + 8]
                    moved = pltpu.roll(block, 4, 0)
                    both = jnp.where(upper, block, moved) if i % 2 == 0 else jnp.where(upper, moved, block)
                    rows = jnp.where(inside, both[None], 0.0).reshape(CY, 128).astype(BF16)
                    row_ref[(2 * i + c) * CY : (2 * i + c + 1) * CY, pl.ds(start, 128)] = rows
            hot_ref[:, pl.ds(start, 128)] = jnp.where(x_cells == x_place, 1.0, 0.0).astype(BF16)
        return carry

    lax.fori_loop(0, SLABS // 4, fill, 0)
    plane = dot(row_ref[0 : 2 * CY, :], hot_ref[...], NT)
    for i in range(1, 4):
        part = dot(row_ref[2 * CY * i : 2 * CY * (i + 1), :], hot_ref[...], NT)
        plane = plane + pltpu.roll(part, i, 1)
    high, low = split(plane)
    table = high_ref[...]
    wave = dot(table, high, NT) + dot(table, low, NT) + dot(low_ref[...], high, NT)
    ac, bc = wave[:NX, :CY], wave[:NX, CY:]
    as_, bs = wave[NX:, :CY], wave[NX:, CY:]

    def put(real, imag):
        real = real.astype(BF16)
        imag = imag.astype(BF16)
        for r in range(PENCILS):
            send_ref[r, 0:LINES, :] = real[r * LINES : (r + 1) * LINES]
            send_ref[r, LINES : 2 * LINES, :] = imag[r * LINES : (r + 1) * LINES]

    @pl.when(place_ref[0] > 0)
    def _():
        put(ac + bs, bc - as_)

    @pl.when(place_ref[0] == 0)
    def _():
        line = iota((NX, CY), 0)
        real = jnp.where(line <= NX // 2, ac, bc)
        imag = jnp.where(line < NX // 2, -as_, -bs)
        put(real, jnp.where((line == 0) | (line == NX // 2), bc, imag))


def quarter(a, b, c, d, sign):
    def add(p, q):
        return (p[0] + q[0], p[1] + q[1])

    def sub(p, q):
        return (p[0] - q[0], p[1] - q[1])

    first, second, third, fourth = add(a, c), sub(a, c), add(b, d), sub(b, d)
    fourth = (-fourth[1], fourth[0]) if sign > 0 else (fourth[1], -fourth[0])
    return [add(first, third), add(second, fourth), sub(first, third), sub(second, fourth)]


def eighth(parts, sign):
    even = quarter(parts[0], parts[2], parts[4], parts[6], sign)
    odd = quarter(parts[1], parts[3], parts[5], parts[7], sign)
    root = math.sqrt(0.5)
    a, b = odd[1]
    odd[1] = ((a - sign * b) * root, (b + sign * a) * root)
    a, b = odd[2]
    odd[2] = (-sign * b, sign * a)
    a, b = odd[3]
    odd[3] = ((-a - sign * b) * root, (sign * a - b) * root)
    return [(e[0] + o[0], e[1] + o[1]) for e, o in zip(even, odd)] + [
        (e[0] - o[0], e[1] - o[1]) for e, o in zip(even, odd)
    ]


def times(value, table):
    high, low = split(value)
    return dot(high, table[0]) + dot(low, table[0]) + dot(high, table[1])


def line_kernel(place_ref, recv_ref, spec_ref, turn_ref, forward_ref, inverse_ref, send_ref):
    special = place_ref[1]
    top = (iota((8, CY), 0) == 0) & (special > 0)
    parts = []
    for q in range(PENCILS):
        real = recv_ref[q, 0:LINES, :].astype(F32)
        imag = recv_ref[q, LINES : 2 * LINES, :].astype(F32)
        first = imag[0:8]
        real = jnp.concatenate([real, jnp.where(top, first, 0.0)], 0)
        imag = jnp.concatenate(
            [jnp.where(top, 0.0, first), imag[8:], jnp.zeros((8, CY), F32)], 0
        )
        parts.append((real, imag))
    parts = eighth(parts, -1)
    lines = []
    for k in range(PENCILS):
        real, imag = parts[k]
        if k > 0:
            c = turn_ref[k : k + 1, :]
            s = turn_ref[PENCILS + k : PENCILS + k + 1, :]
            real, imag = real * c + imag * s, imag * c - real * s
        lines.append(jnp.concatenate([real, imag], 1))
    wave = times(jnp.concatenate(lines, 0), (forward_ref[0], forward_ref[1]))
    spec = spec_ref[...]
    wave = wave * jnp.concatenate([spec, spec], 1)
    wave = times(wave, (inverse_ref[0], inverse_ref[1]))
    parts = []
    for k in range(PENCILS):
        real = wave[k * MORE : (k + 1) * MORE, :CY]
        imag = wave[k * MORE : (k + 1) * MORE, CY:]
        if k > 0:
            c = turn_ref[k : k + 1, :]
            s = turn_ref[PENCILS + k : PENCILS + k + 1, :]
            real, imag = real * c - imag * s, imag * c + real * s
        parts.append((real, imag))
    parts = eighth(parts, 1)
    for q in range(PENCILS):
        real, imag = parts[q]
        send_ref[q] = jnp.concatenate(
            [
                real[0:8] - imag[LINES:],
                real[8:LINES],
                imag[0:8] + real[LINES:],
                imag[8:LINES],
            ],
            0,
        ).astype(BF16)


def sample_kernel(place_ref, pos_ref, recv_ref, high_ref, low_ref, send_ref, left_ref, wave_ref):
    real = jnp.concatenate([recv_ref[r, 0:LINES, :] for r in range(PENCILS)], 0)
    imag = jnp.concatenate([recv_ref[r, LINES : 2 * LINES, :] for r in range(PENCILS)], 0)

    @pl.when(place_ref[0] > 0)
    def _():
        wave_ref[0:NX, 0:CY] = real
        wave_ref[0:NX, CY:] = imag
        wave_ref[NX:, 0:CY] = -imag
        wave_ref[NX:, CY:] = real

    @pl.when(place_ref[0] == 0)
    def _():
        re = real.astype(F32)
        im = imag.astype(F32)
        line = iota((NX, CY), 0)
        ends = (line == 0) | (line == NX // 2)
        low = line < NX // 2
        wave_ref[0:NX, 0:CY] = jnp.where(
            ends, re, jnp.where(low, 2.0 * re, 0.0)
        ).astype(BF16)
        wave_ref[0:NX, CY:] = jnp.where(ends, im, jnp.where(low, 0.0, 2.0 * re)).astype(BF16)
        wave_ref[NX:, 0:CY] = jnp.where(
            ends, 0.0, jnp.where(low, -2.0 * im, 0.0)
        ).astype(BF16)
        wave_ref[NX:, CY:] = jnp.where(ends, 0.0, jnp.where(low, 0.0, -2.0 * im)).astype(BF16)

    cosine, sine = wave_ref[0:NX, :], wave_ref[NX:, :]
    plane = dot(high_ref[0:NX, :], cosine) + dot(high_ref[NX:, :], sine)
    plane = plane + dot(low_ref[0:NX, :], cosine) + dot(low_ref[NX:, :], sine)
    plane = plane.T
    for i in range(4):
        moved = plane if i == 0 else pltpu.roll(plane, NX - i, 1)
        left_ref[2 * CY * i : 2 * CY * (i + 1), :] = moved.astype(BF16)

    x_cells = iota((NX, 128), 0).astype(F32)
    y_cells = (iota((16, 8, 128), 0) * 8 + iota((16, 8, 128), 1)).astype(F32)
    upper = iota((8, 128), 0) < 4
    side = iota((16, 128), 1) < BOX

    def gather(step, carry):
        pairs = [step * 2, step * 2 + 1]
        hot, inside = [], []
        for pair in pairs:
            place = pos_ref[pair]
            hot.append(jnp.where(x_cells == place[0:1], 1.0, 0.0).astype(BF16))
            away = y_cells - place[1:2][None]
            inside.append((away >= 0.0) & (away < 4.0))
        hot = jnp.concatenate(hot, 1)
        found = [[[], []], [[], []]]
        for i in range(4):
            part = dot(left_ref[2 * CY * i : 2 * CY * (i + 1), :], hot)
            for near in range(2):
                for c in range(2):
                    block = part[c * CY : (c + 1) * CY, near * 128 : (near + 1) * 128]
                    block = jnp.where(inside[near], block.reshape(16, 8, 128), 0.0)
                    block = jnp.sum(block, axis=0)
                    found[near][c].append(block + pltpu.roll(block, 4, 0))
        for near in range(2):
            real, imag = [
                jnp.concatenate(
                    [jnp.where(upper, f[0], f[1]), jnp.where(upper, f[2], f[3])], 0
                )
                for f in found[near]
            ]
            pair = pairs[near]
            send_ref[pair * 2] = jnp.where(side, real, pltpu.roll(imag, BOX, 1)).astype(BF16)
            send_ref[pair * 2 + 1] = jnp.where(side, pltpu.roll(real, BOX, 1), imag).astype(BF16)
        return carry

    lax.fori_loop(0, SLABS // 4, gather, 0)


def finish_kernel(meta_ref, phase_ref, recv_ref, proj_ref, close_ref, out_ref, value_ref, wide_ref):
    totals = [jnp.zeros((16, 128), F32) for _ in range(4)]
    for wave in range(SLABS):
        value = recv_ref[wave].astype(F32)
        for k in range(4):
            totals[k] = totals[k] + phase_ref[k, wave : wave + 1, :] * value
    turn = meta_ref[1:2, :] & 3
    row = iota((16, 128), 0) & 3
    for k in range(4):
        value = totals[k] + pltpu.roll(totals[k], BOX, 1)
        out = value
        for m in range(1, 4):
            moved = jnp.where(
                row + m < 4, pltpu.roll(value, 16 - m, 0), pltpu.roll(value, 4 - m, 0)
            )
            out = jnp.where(turn == m, moved, out)
        value_ref[pl.ds(k, 16, stride=4), :] = out
    value = value_ref[...].astype(BF16).astype(F32)
    value = jnp.concatenate([value, value], 0).T[0:BOX]
    box = iota((BOX, 128), 0)
    half = (iota((BOX, 128), 1) >= STENCIL).astype(jnp.int32)
    for m in range(BOX // 2):
        wide_ref[:, 128 * m : 128 * (m + 1)] = jnp.where(
            box == 2 * m + half, value, 0.0
        ).astype(BF16)
    out_ref[...] = dot(wide_ref[...], proj_ref[...]) + close_ref[...]


def near_kernel(ids_ref, group_ref, near_ref, out_ref):
    hot = jnp.where(iota((BOX, GROUP), 1) == ids_ref[...], 1.0, 0.0).astype(BF16)
    partner = dot(hot, group_ref[...]).astype(BF16)
    twice = jnp.concatenate([partner, partner], 0)
    lane = iota((FUNCS, 128), 1) & (BOX - 1)

    def step(index, total):
        start = pl.multiple_of(index * 512, 512)
        part = dot(near_ref[pl.ds(start, 512), :], twice, NT)
        for t in range(4):
            total = jnp.where(lane == index * 4 + t, part[t * FUNCS : (t + 1) * FUNCS], total)
        return total

    total = lax.fori_loop(0, BOX // 4, step, jnp.zeros((FUNCS, 128), F32))
    out_ref[...] = total.T[0:BOX]


VMEM = pl.BlockSpec(memory_space=pltpu.VMEM)
SMEM = pl.BlockSpec(memory_space=pltpu.SMEM)


def call(kernel, shapes, specs, scratch=(), limit=32, flops=0, moved=0):
    return pl.pallas_call(
        kernel,
        out_shape=shapes,
        in_specs=specs,
        out_specs=jax.tree.map(lambda _: VMEM, shapes),
        scratch_shapes=list(scratch),
        compiler_params=pltpu.CompilerParams(vmem_limit_bytes=limit * 1024 * 1024),
        cost_estimate=pl.CostEstimate(flops=flops, bytes_accessed=moved, transcendentals=0),
    )


def struct(*shape, kind=F32):
    return jax.ShapeDtypeStruct(shape, kind)


def project(meta, coefficients, flat):
    return call(
        project_kernel,
        (struct(SLABS, ROWS, 128, kind=BF16), struct(4, SLABS, 128)),
        [VMEM] * 3,
        [pltpu.VMEM((STENCIL, 128), F32)],
        flops=2 * BOXES * FUNCS * 128,
        moved=2 << 20,
    )(meta, coefficients, flat)


def spread(place, received, high, low):
    return call(
        spread_kernel,
        (struct(PENCILS, 2 * LINES, CY, kind=BF16), struct(SLABS // 2, 8, 128)),
        [SMEM] + [VMEM] * 3,
        [pltpu.VMEM((8 * CY, BOXES), BF16), pltpu.VMEM((NX, BOXES), BF16)],
        limit=48,
        flops=2 * BOXES * NX * 8 * CY,
        moved=4 << 20,
    )(place, received, high, low)


def lines(place, received, spec, turn, forward, inverse):
    return call(
        line_kernel,
        struct(PENCILS, 2 * LINES, CY, kind=BF16),
        [SMEM] + [VMEM] * 5,
        flops=2 * 6 * PENCILS * MORE * 256 * 256,
        moved=2 << 20,
    )(place, received, spec, turn, forward, inverse)


def sample(place, pos, received, high, low):
    return call(
        sample_kernel,
        struct(SLABS, 16, 128, kind=BF16),
        [SMEM] + [VMEM] * 4,
        [pltpu.VMEM((8 * CY, NX), BF16), pltpu.VMEM((2 * NX, 2 * CY), BF16)],
        limit=32,
        flops=2 * BOXES * NX * 8 * CY,
        moved=4 << 20,
    )(place, pos, received, high, low)


def finish(meta, phase, received, flat, close):
    return call(
        finish_kernel,
        struct(BOX, FUNCS),
        [VMEM] * 5,
        [pltpu.VMEM((STENCIL, 128), F32), pltpu.VMEM((BOX, BOX * STENCIL), BF16)],
        flops=2 * BOX * BOXES * FUNCS,
        moved=2 << 20,
    )(meta, phase, received, flat, close)


def near(ids, group, blocks):
    return call(
        near_kernel,
        struct(BOX, FUNCS),
        [VMEM] * 3,
        flops=2 * BOX * FUNCS * FUNCS * 128,
        moved=3 << 20,
    )(ids, group, blocks)


def arrange(spectrum, slab, pencil):
    first, second = spectrum[:, 0, :], spectrum[:, 1, :]
    chosen = jnp.where((slab == 0) & (pencil >= PENCILS // 2), second, first)
    head = jnp.where((slab == 0) & (pencil == PENCILS // 2), first[0:1], chosen[0:1])
    rows = jnp.concatenate([head, chosen[1:], jnp.broadcast_to(second[0:1], (8, NY))], 0)
    rows = rows * jnp.where(slab == 0, 1.0, 2.0) * (1.0 / (NX * NY * NZ))
    return rows.reshape(MORE, CY, PENCILS).transpose(2, 0, 1).reshape(PENCILS * MORE, CY)


def describe(anchors, grid_slab):
    def twice(row):
        return jnp.concatenate([row, row])[None]

    x_place = grid_slab[:, 0] * CX + anchors[0]
    place = jnp.concatenate([x_place, anchors[1]])[None]
    return jnp.concatenate(
        [
            twice(anchors[2]),
            twice(anchors[1]),
            jnp.zeros((6, 128), jnp.int32),
            place,
            jnp.zeros((7, 128), jnp.int32),
        ],
        0,
    )


def per_device(coefficients, projection, near_blocks, near_ids, grid_slab, anchors, spectrum):
    slab = lax.axis_index("slab")
    pencil = lax.axis_index("pencil")
    special = (slab == 0) & (pencil % (PENCILS // 2) == 0)
    place = jnp.stack([slab, special.astype(jnp.int32)]).astype(jnp.int32)
    flat = projection.reshape(BOX * STENCIL, FUNCS)
    meta = describe(anchors, grid_slab)
    x_high, x_low = halves(x_table())
    forward, inverse, turn = y_tables()
    forward, inverse = np.stack(halves(forward)), np.stack(halves(inverse))

    send, phase = project(meta, coefficients, flat)
    received = lax.all_to_all(send, "slab", split_axis=0, concat_axis=0, tiled=True)
    spec = arrange(spectrum, slab, pencil)
    group = lax.all_gather(coefficients, "pencil", axis=0, tiled=True)
    close = near(near_ids & (GROUP - 1), group, near_blocks.reshape(BOX * FUNCS, FUNCS))
    send, pos = spread(place, received, x_high, x_low)
    received = lax.all_to_all(send, "pencil", split_axis=0, concat_axis=0, tiled=True)
    send = lines(place, received, spec, turn, forward, inverse)
    received = lax.all_to_all(send, "pencil", split_axis=0, concat_axis=0, tiled=True)
    send = sample(place, pos, received, x_high, x_low)
    received = lax.all_to_all(send, "slab", split_axis=0, concat_axis=0, tiled=True)
    return finish(meta, phase, received, flat, close)


def solution(mesh):
    placed = (
        P(("slab", "pencil"), None),
        P(("slab", "pencil"), None, None),
        P(("slab", "pencil"), None, None, None),
        P(("slab", "pencil"), None),
        P(("slab", "pencil"), None),
        P(None, ("slab", "pencil")),
        P("pencil", "slab", None),
    )
    return jax.shard_map(
        per_device,
        mesh=mesh,
        in_specs=placed,
        out_specs=P(("slab", "pencil"), None),
        check_vma=False,
    )
```

```python
import math

import jax
import jax.numpy as jnp
import numpy as np
from jax import lax
from jax.experimental import pallas as pl
from jax.experimental.pallas import tpu as pltpu
from jax.sharding import PartitionSpec as P

SLABS = 64
PENCILS = 8
BOX = 64
FUNCS = 128
STENCIL = 64
CX = 8
CY = 128
NX = 512
NY = 1024
NZ = 128
GROUP = BOX * PENCILS
ROWS = 24
LINES = NX // PENCILS
MORE = LINES + 8
BOXES = SLABS * BOX
TILE = 256
WINDOW = 48
SHIFT = SLABS - WINDOW
SPAN = CX * WINDOW

F32 = jnp.float32
BF16 = jnp.bfloat16
NT = (((1,), (1,)), ((), ()))
NN = (((1,), (0,)), ((), ()))


def halves(table):
    table = np.asarray(table, np.float32)
    high = table.astype(BF16)
    low = (table - high.astype(np.float32)).astype(BF16)
    return high, low


def x_table():
    half, offset, slab = np.meshgrid(
        np.arange(2), np.arange(CX), np.arange(WINDOW), indexing="ij"
    )
    cells = (CX * (slab + SHIFT * half) + offset).reshape(-1)
    phase = np.outer(np.arange(NX), cells) % NX * (2.0 * math.pi / NX)
    return np.concatenate([np.cos(phase), np.sin(phase)], 0)


def y_tables():
    phase = np.outer(np.arange(CY), np.arange(CY)) % CY * (2.0 * math.pi / CY)
    c, s = np.cos(phase), np.sin(phase)
    forward = np.block([[c, -s], [s, c]])
    inverse = np.block([[c, s], [-s, c]])
    turn = np.outer(np.arange(PENCILS), np.arange(CY)) * (2.0 * math.pi / NY)
    turn = np.concatenate([np.cos(turn), np.sin(turn)], 0).astype(np.float32)
    return forward, inverse, turn


def cosine_coefficients():
    fit = np.polynomial.chebyshev.Chebyshev.interpolate(
        lambda w: np.cos(2.0 * math.pi * np.sqrt(w)), 9, domain=[0.0, 0.25]
    )
    return [float(v) for v in fit.convert(kind=np.polynomial.Polynomial).coef]


COSINE = cosine_coefficients()


def cosine_of(step):
    u = (step.astype(F32) - (NZ // 2)) * (1.0 / NZ)
    w = u * u
    total = jnp.full_like(w, COSINE[-1])
    for value in COSINE[-2::-1]:
        total = total * w + value
    return -total


def iota(shape, axis):
    return lax.broadcasted_iota(jnp.int32, shape, axis)


def dot(a, b, dims=NN):
    return lax.dot_general(a, b, dims, preferred_element_type=F32)


def split(value):
    high = value.astype(BF16)
    return high, (value - high.astype(F32)).astype(BF16)


def swap(first, other, width):
    even = iota(first.shape, 1) & width == 0
    return (
        jnp.where(even, first, pltpu.roll(other, width, 1)),
        jnp.where(even, pltpu.roll(first, 128 - width, 1), other),
    )


def regroup(tiles):
    a, c = swap(tiles[0], tiles[2], 64)
    b, d = swap(tiles[1], tiles[3], 64)
    return swap(a, b, 32) + swap(c, d, 32)


def ungroup(tiles):
    a, b = swap(tiles[0], tiles[1], 32)
    c, d = swap(tiles[2], tiles[3], 32)
    first, third = swap(a, c, 64)
    second, fourth = swap(b, d, 64)
    return first, second, third, fourth


def project_kernel(
    anchor_hbm, slab_hbm, coef_hbm, proj_hbm,
    send_ref, phase_ref, turn_ref, back_ref,
    value_ref, anchor_ref, slab_ref, coef_ref, proj_ref, sems,
):
    count = 4
    size = BOX * STENCIL // count
    small = [
        pltpu.make_async_copy(source, target, sems.at[n])
        for n, (source, target) in enumerate(
            ((slab_hbm, slab_ref), (anchor_hbm, anchor_ref), (coef_hbm, coef_ref))
        )
    ]
    for copy in small:
        copy.start()
    large = [
        pltpu.make_async_copy(
            proj_hbm.at[n * size : (n + 1) * size, :],
            proj_ref.at[n * size : (n + 1) * size, :],
            sems.at[3 + n],
        )
        for n in range(count)
    ]
    for copy in large:
        copy.start()
    for copy in small:
        copy.wait()

    slab = slab_ref[...].astype(F32)
    box = iota((1, BOX), 1).astype(F32)
    key = slab * BOX + box
    key = jnp.concatenate([key, key], 1)
    column = jnp.broadcast_to(key, (128, 128)).T[0:BOX]
    rank = jnp.sum(jnp.where(column < key, 1.0, 0.0), axis=0, keepdims=True)
    column = jnp.broadcast_to(rank, (128, 128)).T[0:BOX]
    lane = (iota((BOX, 128), 1) & (BOX - 1)).astype(F32)
    chosen = column == lane
    order = jnp.sum(
        jnp.where(chosen, iota((BOX, 128), 0).astype(F32), 0.0), axis=0, keepdims=True
    )
    row = iota((128, 128), 0)
    hot = jnp.where((row & (BOX - 1)).astype(F32) == rank, 1.0, 0.0)
    back_ref[...] = jnp.where(row < BOX, hot, 0.0).astype(BF16)
    twice = dot(hot.astype(BF16)[:, 0:BOX], coef_ref[...]).astype(BF16)
    table = jnp.concatenate(
        [anchor_ref[...].astype(F32), slab, jnp.zeros((4, BOX), F32)], 0
    ).astype(BF16)
    table = dot(table, jnp.where(chosen, 1.0, 0.0).astype(BF16))
    later = (iota((1, 128), 1) & (BOX // 2) > 0).astype(F32)
    code = table[0:1] * WINDOW + table[3:4] - later * SHIFT
    y_place = table[1:2]
    depth = table[2:3].astype(jnp.int32)
    turn_ref[...] = jnp.broadcast_to(y_place, (8, 128))

    second = (iota((SLABS, 128), 1) >= BOX).astype(jnp.int32)
    wave = iota((SLABS, 128), 0)
    for k in range(4):
        z = depth + k
        step = jnp.where(wave == 0, second * (NZ // 2) * z, wave * z + second * (NZ // 4))
        phase_ref[k] = cosine_of(step & (NZ - 1))

    total = jnp.zeros((STENCIL, 128), F32)
    per = TILE // STENCIL
    for block in range(BOX // per):
        if block * count % (BOX // per) == 0:
            large[block * count // (BOX // per)].wait()
        part = dot(proj_ref[block * TILE : (block + 1) * TILE, :], twice, NT)
        for t in range(per):
            mine = order == float(block * per + t)
            total = jnp.where(mine, part[t * STENCIL : (t + 1) * STENCIL], total)
    value_ref[...] = total

    turn = y_place.astype(jnp.int32) & 3
    row = iota((16, 128), 0) & 3
    parts = []
    for k in range(4):
        value = value_ref[pl.ds(k, 16, stride=4), :]
        out = value
        for m in range(1, 4):
            moved = jnp.where(row >= m, pltpu.roll(value, m, 0), pltpu.roll(value, m + 12, 0))
            out = jnp.where(turn == m, moved, out)
        parts.append(out)
    places = jnp.where(iota((8, 128), 1) < BOX, code, y_place)
    for wave in range(SLABS):
        total = phase_ref[0, wave : wave + 1, :] * parts[0]
        for k in range(1, 4):
            total = total + phase_ref[k, wave : wave + 1, :] * parts[k]
        send_ref[wave] = jnp.concatenate([total, places], 0).astype(BF16)


def spread_kernel(place_ref, recv_ref, table_ref, send_ref, pos_ref, row_ref, hot_ref):
    cells = iota((TILE, 128), 0).astype(F32)
    y_cells = iota((CY, 128), 0).astype(F32)
    upper = iota((8, 128), 0) < 4

    groups = []
    for step in range(SLABS // 4):
        tiles = regroup([recv_ref[step * 4 + n].astype(F32) for n in range(4)])
        groups.append(((tiles[0], tiles[2]), (tiles[1], tiles[3])))
        places = [tile[16:17] for pair in groups[-1] for tile in pair]
        pos_ref[step] = jnp.concatenate(places + [jnp.zeros((4, 128), F32)], 0)

    def fill(step, half):
        real, imag = groups[step][half]
        code, y_place = real[16:17], imag[16:17]
        start = half * (BOXES // 2) + step * 128
        away = y_cells - y_place
        inside = jnp.where((away >= 0.0) & (away < 4.0), 1.0, 0.0).astype(BF16)
        inside = inside.reshape(8, 16, 128)
        for i in range(4):
            for c, source in enumerate((real, imag)):
                block = source[8 * (i // 2) : 8 * (i // 2) + 8]
                moved = pltpu.roll(block, 4, 0)
                pair = (block, moved) if i % 2 == 0 else (moved, block)
                both = jnp.where(upper, pair[0], pair[1])
                both = jnp.concatenate([both, both], 0).astype(BF16)
                rows = (inside * both[None]).reshape(CY, 128)
                row_ref[(2 * i + c) * CY : (2 * i + c + 1) * CY, start : start + 128] = rows
        hot_ref[:, start : start + 128] = jnp.where(cells == code, 1.0, 0.0).astype(BF16)

    planes = []
    for half in range(2):
        for step in range(SLABS // 4):
            fill(step, half)
        lanes = slice(half * (BOXES // 2), (half + 1) * (BOXES // 2))
        plane = None
        for i in range(4):
            part = dot(row_ref[2 * CY * i : 2 * CY * (i + 1), lanes], hot_ref[:, lanes], NT)
            part = jnp.concatenate([part, jnp.zeros((2 * CY, SPAN - TILE), F32)], 1)
            plane = part if i == 0 else plane + pltpu.roll(part, WINDOW * i, 1)
        planes.append(plane)
    wave = dot(table_ref[...], jnp.concatenate(planes, 1).astype(BF16), NT)
    ac, bc = wave[:NX, :CY], wave[:NX, CY:]
    as_, bs = wave[NX:, :CY], wave[NX:, CY:]

    def put(real, imag):
        real = real.astype(BF16)
        imag = imag.astype(BF16)
        for r in range(PENCILS):
            send_ref[r, 0:LINES, :] = real[r * LINES : (r + 1) * LINES]
            send_ref[r, LINES : 2 * LINES, :] = imag[r * LINES : (r + 1) * LINES]

    @pl.when(place_ref[0] > 0)
    def _():
        put(ac + bs, bc - as_)

    @pl.when(place_ref[0] == 0)
    def _():
        line = iota((NX, CY), 0)
        real = jnp.where(line <= NX // 2, ac, bc)
        imag = jnp.where(line < NX // 2, -as_, -bs)
        put(real, jnp.where((line == 0) | (line == NX // 2), bc, imag))


def quarter(a, b, c, d, sign):
    def add(p, q):
        return (p[0] + q[0], p[1] + q[1])

    def sub(p, q):
        return (p[0] - q[0], p[1] - q[1])

    first, second, third, fourth = add(a, c), sub(a, c), add(b, d), sub(b, d)
    fourth = (-fourth[1], fourth[0]) if sign > 0 else (fourth[1], -fourth[0])
    return [add(first, third), add(second, fourth), sub(first, third), sub(second, fourth)]


def eighth(parts, sign):
    even = quarter(parts[0], parts[2], parts[4], parts[6], sign)
    odd = quarter(parts[1], parts[3], parts[5], parts[7], sign)
    root = math.sqrt(0.5)
    a, b = odd[1]
    odd[1] = ((a - sign * b) * root, (b + sign * a) * root)
    a, b = odd[2]
    odd[2] = (-sign * b, sign * a)
    a, b = odd[3]
    odd[3] = ((-a - sign * b) * root, (sign * a - b) * root)
    return [(e[0] + o[0], e[1] + o[1]) for e, o in zip(even, odd)] + [
        (e[0] - o[0], e[1] - o[1]) for e, o in zip(even, odd)
    ]


def times(value, table):
    high, low = split(value)
    return dot(high, table[0]) + dot(low, table[0]) + dot(high, table[1])


def line_kernel(place_ref, recv_ref, spec_ref, turn_ref, forward_ref, inverse_ref, send_ref):
    special = place_ref[1]
    top = (iota((8, CY), 0) == 0) & (special > 0)
    parts = []
    for q in range(PENCILS):
        real = recv_ref[q, 0:LINES, :].astype(F32)
        imag = recv_ref[q, LINES : 2 * LINES, :].astype(F32)
        first = imag[0:8]
        real = jnp.concatenate([real, jnp.where(top, first, 0.0)], 0)
        imag = jnp.concatenate(
            [jnp.where(top, 0.0, first), imag[8:], jnp.zeros((8, CY), F32)], 0
        )
        parts.append((real, imag))
    parts = eighth(parts, -1)
    lines = []
    for k in range(PENCILS):
        real, imag = parts[k]
        if k > 0:
            c = turn_ref[k : k + 1, :]
            s = turn_ref[PENCILS + k : PENCILS + k + 1, :]
            real, imag = real * c + imag * s, imag * c - real * s
        lines.append(jnp.concatenate([real, imag], 1))
    wave = times(jnp.concatenate(lines, 0), (forward_ref[0], forward_ref[1]))
    spec = spec_ref[...]
    wave = wave * jnp.concatenate([spec, spec], 1)
    wave = times(wave, (inverse_ref[0], inverse_ref[1]))
    parts = []
    for k in range(PENCILS):
        real = wave[k * MORE : (k + 1) * MORE, :CY]
        imag = wave[k * MORE : (k + 1) * MORE, CY:]
        if k > 0:
            c = turn_ref[k : k + 1, :]
            s = turn_ref[PENCILS + k : PENCILS + k + 1, :]
            real, imag = real * c - imag * s, imag * c + real * s
        parts.append((real, imag))
    parts = eighth(parts, 1)
    for q in range(PENCILS):
        real, imag = parts[q]
        send_ref[q] = jnp.concatenate(
            [
                real[0:8] - imag[LINES:],
                real[8:LINES],
                imag[0:8] + real[LINES:],
                imag[8:LINES],
            ],
            0,
        ).astype(BF16)


def sample_kernel(place_ref, pos_ref, recv_ref, table_ref, send_ref, left_ref, wave_ref):
    real = jnp.concatenate([recv_ref[r, 0:LINES, :] for r in range(PENCILS)], 0)
    imag = jnp.concatenate([recv_ref[r, LINES : 2 * LINES, :] for r in range(PENCILS)], 0)
    real = real.astype(F32).T
    imag = imag.astype(F32).T

    def put(first, second, third, fourth):
        wave_ref[0:CY, 0:NX] = first.astype(BF16)
        wave_ref[0:CY, NX:] = second.astype(BF16)
        wave_ref[CY:, 0:NX] = third.astype(BF16)
        wave_ref[CY:, NX:] = fourth.astype(BF16)

    @pl.when(place_ref[0] > 0)
    def _():
        put(real, -imag, imag, real)

    @pl.when(place_ref[0] == 0)
    def _():
        line = iota((CY, NX), 1)
        ends = (line == 0) | (line == NX // 2)
        low = line < NX // 2
        put(
            jnp.where(ends, real, jnp.where(low, 2.0 * real, 0.0)),
            jnp.where(ends, 0.0, jnp.where(low, -2.0 * imag, 0.0)),
            jnp.where(ends, imag, jnp.where(low, 0.0, 2.0 * real)),
            jnp.where(ends, 0.0, jnp.where(low, 0.0, -2.0 * imag)),
        )

    plane = dot(wave_ref[...], table_ref[...])
    for half in range(2):
        part = plane[:, half * SPAN : (half + 1) * SPAN]
        for i in range(4):
            moved = part if i == 0 else pltpu.roll(part, SPAN - WINDOW * i, 1)
            left_ref[half, 2 * CY * i : 2 * CY * (i + 1), :] = moved[:, :TILE].astype(BF16)

    cells = iota((TILE, 128), 0).astype(F32)
    y_cells = (iota((16, 8, 128), 0) * 8 + iota((16, 8, 128), 1)).astype(F32)
    upper = iota((8, 128), 0) < 4

    def gather(step):
        quads = [step * 2, step * 2 + 1]
        found = {}
        for half in range(2):
            hot, inside = [], []
            for quad in quads:
                place = pos_ref[quad]
                code, y_place = place[2 * half : 2 * half + 1], place[2 * half + 1 : 2 * half + 2]
                hot.append(jnp.where(cells == code, 1.0, 0.0).astype(BF16))
                away = y_cells - y_place[None]
                inside.append((away >= 0.0) & (away < 4.0))
            hot = jnp.concatenate(hot, 1)
            for i in range(4):
                part = dot(left_ref[half, 2 * CY * i : 2 * CY * (i + 1), :], hot)
                for near in range(2):
                    for c in range(2):
                        block = part[c * CY : (c + 1) * CY, near * 128 : (near + 1) * 128]
                        block = jnp.where(inside[near], block.reshape(16, 8, 128), 0.0)
                        block = jnp.sum(block, axis=0)
                        found[near, c, half, i] = block + pltpu.roll(block, 4, 0)
        for near in range(2):
            tiles = []
            for c in range(2):
                for half in range(2):
                    f = [found[near, c, half, i] for i in range(4)]
                    tiles.append(
                        jnp.concatenate(
                            [jnp.where(upper, f[0], f[1]), jnp.where(upper, f[2], f[3])], 0
                        )
                    )
            for n, tile in enumerate(ungroup(tiles)):
                send_ref[quads[near] * 4 + n] = tile.astype(BF16)

    for step in range(SLABS // 8):
        gather(step)


def finish_kernel(
    turn_ref, back_ref, phase_ref, recv_ref, close_ref, proj_ref, out_ref, value_ref, wide_ref
):
    totals = [jnp.zeros((16, 128), F32) for _ in range(4)]
    for wave in range(SLABS):
        value = recv_ref[wave].astype(F32)
        for k in range(4):
            totals[k] = totals[k] + phase_ref[k, wave : wave + 1, :] * value
    turn = turn_ref[0:1, :].astype(jnp.int32) & 3
    row = iota((16, 128), 0) & 3
    for k in range(4):
        value = totals[k] + pltpu.roll(totals[k], BOX, 1)
        out = value
        for m in range(1, 4):
            moved = jnp.where(
                row + m < 4, pltpu.roll(value, 16 - m, 0), pltpu.roll(value, 4 - m, 0)
            )
            out = jnp.where(turn == m, moved, out)
        value_ref[pl.ds(k, 16, stride=4), :] = out
    value = dot(value_ref[...].astype(BF16), back_ref[...])
    value = jnp.concatenate([value, value], 0).T[0:BOX]
    box = iota((BOX, 128), 0)
    half = (iota((BOX, 128), 1) >= STENCIL).astype(jnp.int32)
    for m in range(BOX // 2):
        wide_ref[:, 128 * m : 128 * (m + 1)] = jnp.where(
            box == 2 * m + half, value, 0.0
        ).astype(BF16)
    out_ref[...] = dot(wide_ref[...], proj_ref[...]) + close_ref[...]


def near_kernel(ids_ref, group_ref, near_ref, out_ref):
    hot = jnp.where(iota((BOX, GROUP), 1) == ids_ref[...], 1.0, 0.0).astype(BF16)
    partner = dot(hot, group_ref[...]).astype(BF16)
    twice = jnp.concatenate([partner, partner], 0)
    lane = iota((FUNCS, 128), 1) & (BOX - 1)

    def step(index, total):
        start = pl.multiple_of(index * 512, 512)
        part = dot(near_ref[pl.ds(start, 512), :], twice, NT)
        for t in range(4):
            total = jnp.where(lane == index * 4 + t, part[t * FUNCS : (t + 1) * FUNCS], total)
        return total

    total = lax.fori_loop(0, BOX // 4, step, jnp.zeros((FUNCS, 128), F32))
    out_ref[...] = total.T[0:BOX]


VMEM = pl.BlockSpec(memory_space=pltpu.VMEM)
SMEM = pl.BlockSpec(memory_space=pltpu.SMEM)
HBM = pl.BlockSpec(memory_space=pltpu.HBM)


def call(kernel, shapes, specs, scratch=(), limit=32, flops=0, moved=0):
    return pl.pallas_call(
        kernel,
        out_shape=shapes,
        in_specs=specs,
        out_specs=jax.tree.map(lambda _: VMEM, shapes),
        scratch_shapes=list(scratch),
        compiler_params=pltpu.CompilerParams(vmem_limit_bytes=limit * 1024 * 1024),
        cost_estimate=pl.CostEstimate(flops=flops, bytes_accessed=moved, transcendentals=0),
    )


def resident(*arrays):
    return [pltpu.with_memory_space_constraint(a, pltpu.HBM) for a in arrays]


def struct(*shape, kind=F32):
    return jax.ShapeDtypeStruct(shape, kind)


def project(anchors, slabs, coefficients, flat):
    return call(
        project_kernel,
        (
            struct(SLABS, ROWS, 128, kind=BF16),
            struct(4, SLABS, 128),
            struct(8, 128),
            struct(128, 128, kind=BF16),
        ),
        [HBM] * 4,
        [
            pltpu.VMEM((STENCIL, 128), F32),
            pltpu.VMEM(anchors.shape, jnp.int32),
            pltpu.VMEM(slabs.shape, jnp.int32),
            pltpu.VMEM(coefficients.shape, BF16),
            pltpu.VMEM(flat.shape, BF16),
            pltpu.SemaphoreType.DMA((7,)),
        ],
        limit=8,
        flops=2 * BOXES * FUNCS * 128,
        moved=2 << 20,
    )(*resident(anchors, slabs, coefficients, flat))


def spread(place, received, table):
    return call(
        spread_kernel,
        (struct(PENCILS, 2 * LINES, CY, kind=BF16), struct(SLABS // 4, 8, 128)),
        [SMEM] + [VMEM] * 2,
        [pltpu.VMEM((8 * CY, BOXES), BF16), pltpu.VMEM((TILE, BOXES), BF16)],
        limit=28,
        flops=2 * BOXES * TILE * 8 * CY,
        moved=4 << 20,
    )(place, received, table)


def lines(place, received, spec, turn, forward, inverse):
    return call(
        line_kernel,
        struct(PENCILS, 2 * LINES, CY, kind=BF16),
        [SMEM] + [VMEM] * 5,
        limit=12,
        flops=2 * 6 * PENCILS * MORE * 256 * 256,
        moved=2 << 20,
    )(place, received, spec, turn, forward, inverse)


def sample(place, pos, received, table):
    return call(
        sample_kernel,
        struct(SLABS, 16, 128, kind=BF16),
        [SMEM] + [VMEM] * 3,
        [pltpu.VMEM((2, 8 * CY, TILE), BF16), pltpu.VMEM((2 * CY, 2 * NX), BF16)],
        limit=16,
        flops=2 * BOXES * TILE * 8 * CY,
        moved=4 << 20,
    )(place, pos, received, table)


def finish(turn, back, phase, received, close, flat):
    return call(
        finish_kernel,
        struct(BOX, FUNCS),
        [VMEM] * 6,
        [pltpu.VMEM((STENCIL, 128), F32), pltpu.VMEM((BOX, BOX * STENCIL), BF16)],
        limit=8,
        flops=2 * BOX * BOXES * FUNCS,
        moved=2 << 20,
    )(turn, back, phase, received, close, flat)


def near(ids, group, blocks):
    return call(
        near_kernel,
        struct(BOX, FUNCS),
        [VMEM] * 3,
        limit=8,
        flops=2 * BOX * FUNCS * FUNCS * 128,
        moved=3 << 20,
    )(ids, group, blocks)


def arrange(spectrum, slab, pencil):
    first, second = spectrum[:, 0, :], spectrum[:, 1, :]
    chosen = jnp.where((slab == 0) & (pencil >= PENCILS // 2), second, first)
    head = jnp.where((slab == 0) & (pencil == PENCILS // 2), first[0:1], chosen[0:1])
    rows = jnp.concatenate([head, chosen[1:], jnp.broadcast_to(second[0:1], (8, NY))], 0)
    rows = rows * jnp.where(slab == 0, 1.0, 2.0) * (1.0 / (NX * NY * NZ))
    return rows.reshape(MORE, CY, PENCILS).transpose(2, 0, 1).reshape(PENCILS * MORE, CY)


def per_device(coefficients, projection, near_blocks, near_ids, grid_slab, anchors, spectrum):
    slab = lax.axis_index("slab")
    pencil = lax.axis_index("pencil")
    special = (slab == 0) & (pencil % (PENCILS // 2) == 0)
    place = jnp.stack([slab, special.astype(jnp.int32)]).astype(jnp.int32)
    flat = projection.reshape(BOX * STENCIL, FUNCS)
    table = jnp.asarray(x_table().astype(BF16))
    forward, inverse, turn = y_tables()
    forward, inverse = np.stack(halves(forward)), np.stack(halves(inverse))

    send, phase, turned, back = project(anchors, grid_slab.reshape(1, BOX), coefficients, flat)
    received = lax.all_to_all(send, "slab", split_axis=0, concat_axis=0, tiled=True)
    spec = arrange(spectrum, slab, pencil)
    group = lax.all_gather(coefficients, "pencil", axis=0, tiled=True)
    close = near(near_ids & (GROUP - 1), group, near_blocks.reshape(BOX * FUNCS, FUNCS))
    received, spec, place = lax.optimization_barrier((received, spec, place))
    send, pos = spread(place, received, table)
    received = lax.all_to_all(send, "pencil", split_axis=0, concat_axis=0, tiled=True)
    send = lines(place, received, spec, turn, forward, inverse)
    received = lax.all_to_all(send, "pencil", split_axis=0, concat_axis=0, tiled=True)
    send = sample(place, pos, received, table)
    received = lax.all_to_all(send, "slab", split_axis=0, concat_axis=0, tiled=True)
    return finish(turned, back, phase, received, close, flat)


def solution(mesh):
    placed = (
        P(("slab", "pencil"), None),
        P(("slab", "pencil"), None, None),
        P(("slab", "pencil"), None, None, None),
        P(("slab", "pencil"), None),
        P(("slab", "pencil"), None),
        P(None, ("slab", "pencil")),
        P("pencil", "slab", None),
    )
    return jax.shard_map(
        per_device,
        mesh=mesh,
        in_specs=placed,
        out_specs=P(("slab", "pencil"), None),
        check_vma=False,
    )
```

```python
import math

import jax
import jax.numpy as jnp
import numpy as np
from jax import lax
from jax.experimental import pallas as pl
from jax.experimental.pallas import tpu as pltpu
from jax.sharding import PartitionSpec as P

SLABS = 64
PENCILS = 8
BOX = 64
FUNCS = 128
STENCIL = 64
CX = 8
CY = 128
NX = 512
NY = 1024
NZ = 128
GROUP = BOX * PENCILS
ROWS = 18
LINES = NX // PENCILS
MORE = LINES + 8
BOXES = SLABS * BOX
SMALL = 8 + 128
SIDE = BOX + 128
TILE = 256
WINDOW = 48
SHIFT = SLABS - WINDOW
SPAN = CX * WINDOW

F32 = jnp.float32
BF16 = jnp.bfloat16
NT = (((1,), (1,)), ((), ()))
NN = (((1,), (0,)), ((), ()))


def halves(table):
    table = np.asarray(table, np.float32)
    high = table.astype(BF16)
    low = (table - high.astype(np.float32)).astype(BF16)
    return high, low


def x_table():
    half, offset, slab = np.meshgrid(
        np.arange(2), np.arange(CX), np.arange(WINDOW), indexing="ij"
    )
    cells = (CX * (slab + SHIFT * half) + offset).reshape(-1)
    phase = np.outer(np.arange(NX), cells) % NX * (2.0 * math.pi / NX)
    return np.concatenate([np.cos(phase), np.sin(phase)], 0)


def y_tables():
    phase = np.outer(np.arange(CY), np.arange(CY)) % CY * (2.0 * math.pi / CY)
    c, s = np.cos(phase), np.sin(phase)
    forward = np.block([[c, -s], [s, c]])
    inverse = np.block([[c, s], [-s, c]])
    turn = np.outer(np.arange(PENCILS), np.arange(CY)) * (2.0 * math.pi / NY)
    turn = np.concatenate([np.cos(turn), np.sin(turn)], 0).astype(np.float32)
    return forward, inverse, turn


def cosine_coefficients():
    fit = np.polynomial.chebyshev.Chebyshev.interpolate(
        lambda w: np.cos(2.0 * math.pi * np.sqrt(w)), 9, domain=[0.0, 0.25]
    )
    return [float(v) for v in fit.convert(kind=np.polynomial.Polynomial).coef]


COSINE = cosine_coefficients()


def cosine_of(step):
    u = (step.astype(F32) - (NZ // 2)) * (1.0 / NZ)
    w = u * u
    total = jnp.full_like(w, COSINE[-1])
    for value in COSINE[-2::-1]:
        total = total * w + value
    return -total


def iota(shape, axis):
    return lax.broadcasted_iota(jnp.int32, shape, axis)


def dot(a, b, dims=NN):
    return lax.dot_general(a, b, dims, preferred_element_type=F32)


def split(value):
    high = value.astype(BF16)
    return high, (value - high.astype(F32)).astype(BF16)


def swap(first, other, width):
    even = iota(first.shape, 1) & width == 0
    return (
        jnp.where(even, first, pltpu.roll(other, width, 1)),
        jnp.where(even, pltpu.roll(first, 128 - width, 1), other),
    )


def regroup(tiles):
    a, c = swap(tiles[0], tiles[2], 64)
    b, d = swap(tiles[1], tiles[3], 64)
    return swap(a, b, 32) + swap(c, d, 32)


def ungroup(tiles):
    a, b = swap(tiles[0], tiles[1], 32)
    c, d = swap(tiles[2], tiles[3], 32)
    first, third = swap(a, c, 64)
    second, fourth = swap(b, d, 64)
    return first, second, third, fourth


def phases(depth, phase_ref):
    second = (iota((SLABS, 128), 1) >= BOX).astype(jnp.int32)
    wave = iota((SLABS, 128), 0)
    for k in range(4):
        z = depth + k
        step = jnp.where(wave == 0, second * (NZ // 2) * z, wave * z + second * (NZ // 4))
        phase_ref[k * SLABS : (k + 1) * SLABS] = cosine_of(step & (NZ - 1))


def project_kernel(
    anchor_hbm, slab_hbm, coef_hbm, proj_hbm,
    send_hbm, small_hbm,
    send_ref, small_ref, phase_ref, value_ref, anchor_ref, slab_ref, coef_ref, proj_ref, sems,
):
    count = 4
    size = BOX * STENCIL // count
    small = [
        pltpu.make_async_copy(source, target, sems.at[n])
        for n, (source, target) in enumerate(
            ((slab_hbm, slab_ref), (anchor_hbm, anchor_ref), (coef_hbm, coef_ref))
        )
    ]
    for copy in small:
        copy.start()
    large = [
        pltpu.make_async_copy(
            proj_hbm.at[n * size : (n + 1) * size, :],
            proj_ref.at[n * size : (n + 1) * size, :],
            sems.at[3 + n],
        )
        for n in range(count)
    ]
    for copy in large:
        copy.start()
    for copy in small:
        copy.wait()

    slab = slab_ref[...].astype(F32)
    box = iota((1, BOX), 1).astype(F32)
    key = slab * BOX + box
    key = jnp.concatenate([key, key], 1)
    column = jnp.broadcast_to(key, (128, 128)).T[0:BOX]
    rank = jnp.sum(jnp.where(column < key, 1.0, 0.0), axis=0, keepdims=True)
    column = jnp.broadcast_to(rank, (128, 128)).T[0:BOX]
    lane = (iota((BOX, 128), 1) & (BOX - 1)).astype(F32)
    chosen = column == lane
    order = jnp.sum(
        jnp.where(chosen, iota((BOX, 128), 0).astype(F32), 0.0), axis=0, keepdims=True
    )
    row = iota((128, 128), 0)
    hot = jnp.where((row & (BOX - 1)).astype(F32) == rank, 1.0, 0.0)
    twice = dot(hot.astype(BF16)[:, 0:BOX], coef_ref[...]).astype(BF16)
    table = jnp.concatenate(
        [anchor_ref[...].astype(F32), slab, jnp.zeros((4, BOX), F32)], 0
    ).astype(BF16)
    table = dot(table, jnp.where(chosen, 1.0, 0.0).astype(BF16))
    later = (iota((1, 128), 1) & (BOX // 2) > 0).astype(F32)
    code = table[0:1] * WINDOW + table[3:4] - later * SHIFT
    y_place = table[1:2]
    depth = table[2:3].astype(jnp.int32)
    small_ref[0:8] = jnp.concatenate([y_place, table[2:3], jnp.zeros((6, 128), F32)], 0)
    small_ref[8:] = jnp.where(row < BOX, hot, 0.0)
    notes = pltpu.make_async_copy(small_ref, small_hbm, sems.at[11])
    notes.start()
    phases(depth, phase_ref)

    total = jnp.zeros((STENCIL, 128), F32)
    per = TILE // STENCIL
    for block in range(BOX // per):
        if block * count % (BOX // per) == 0:
            large[block * count // (BOX // per)].wait()
        part = dot(proj_ref[block * TILE : (block + 1) * TILE, :], twice, NT)
        for t in range(per):
            mine = order == float(block * per + t)
            total = jnp.where(mine, part[t * STENCIL : (t + 1) * STENCIL], total)
    value_ref[...] = total

    turn = y_place.astype(jnp.int32) & 3
    row = iota((16, 128), 0) & 3
    parts = []
    for k in range(4):
        value = value_ref[pl.ds(k, 16, stride=4), :]
        out = value
        for m in range(1, 4):
            moved = jnp.where(row >= m, pltpu.roll(value, m, 0), pltpu.roll(value, m + 12, 0))
            out = jnp.where(turn == m, moved, out)
        parts.append(out)
    places = jnp.where(iota((8, 128), 1) < BOX, code, y_place)[0 : ROWS - 16]
    size = SLABS // count
    copies = []
    for wave in range(SLABS):
        total = phase_ref[wave : wave + 1, :] * parts[0]
        for k in range(1, 4):
            row = k * SLABS + wave
            total = total + phase_ref[row : row + 1, :] * parts[k]
        total = jnp.concatenate([total, places], 0).reshape(ROWS // 2, 2, 128)
        send_ref[wave] = total.astype(BF16)
        if wave % size == size - 1:
            n = wave // size
            copies.append(
                pltpu.make_async_copy(
                    send_ref.at[n * size : (n + 1) * size],
                    send_hbm.at[n * size : (n + 1) * size],
                    sems.at[7 + n],
                )
            )
            copies[-1].start()
    for copy in copies:
        copy.wait()
    notes.wait()


def spread_kernel(place_ref, recv_ref, table_ref, send_ref, pos_ref, row_ref, hot_ref):
    cells = iota((TILE, 128), 0).astype(F32)
    y_cells = iota((CY, 128), 0).astype(F32)
    upper = iota((8, 128), 0) < 4

    groups = []
    for step in range(SLABS // 4):
        tiles = []
        for n in range(4):
            tile = recv_ref[step * 4 + n].astype(F32).reshape(ROWS, 128)
            tiles.append(jnp.concatenate([tile, jnp.zeros((24 - ROWS, 128), F32)], 0))
        tiles = regroup(tiles)
        groups.append(((tiles[0], tiles[2]), (tiles[1], tiles[3])))
        places = [tile[16:17] for pair in groups[-1] for tile in pair]
        pos_ref[step] = jnp.concatenate(places + [jnp.zeros((4, 128), F32)], 0)

    def fill(step, half):
        real, imag = groups[step][half]
        code, y_place = real[16:17], imag[16:17]
        start = half * (BOXES // 2) + step * 128
        away = y_cells - y_place
        inside = jnp.where((away >= 0.0) & (away < 4.0), 1.0, 0.0).astype(BF16)
        inside = inside.reshape(8, 16, 128)
        for i in range(4):
            for c, source in enumerate((real, imag)):
                block = source[8 * (i // 2) : 8 * (i // 2) + 8]
                moved = pltpu.roll(block, 4, 0)
                pair = (block, moved) if i % 2 == 0 else (moved, block)
                both = jnp.where(upper, pair[0], pair[1])
                both = jnp.concatenate([both, both], 0).astype(BF16)
                rows = (inside * both[None]).reshape(CY, 128)
                row_ref[(2 * i + c) * CY : (2 * i + c + 1) * CY, start : start + 128] = rows
        hot_ref[:, start : start + 128] = jnp.where(cells == code, 1.0, 0.0).astype(BF16)

    planes = []
    for half in range(2):
        for step in range(SLABS // 4):
            fill(step, half)
        lanes = slice(half * (BOXES // 2), (half + 1) * (BOXES // 2))
        plane = None
        for i in range(4):
            part = dot(row_ref[2 * CY * i : 2 * CY * (i + 1), lanes], hot_ref[:, lanes], NT)
            part = jnp.concatenate([part, jnp.zeros((2 * CY, SPAN - TILE), F32)], 1)
            plane = part if i == 0 else plane + pltpu.roll(part, WINDOW * i, 1)
        planes.append(plane)
    wave = dot(table_ref[...], jnp.concatenate(planes, 1).astype(BF16), NT)
    ac, bc = wave[:NX, :CY], wave[:NX, CY:]
    as_, bs = wave[NX:, :CY], wave[NX:, CY:]

    def put(real, imag):
        real = real.astype(BF16)
        imag = imag.astype(BF16)
        for r in range(PENCILS):
            send_ref[r, 0:LINES, :] = real[r * LINES : (r + 1) * LINES]
            send_ref[r, LINES : 2 * LINES, :] = imag[r * LINES : (r + 1) * LINES]

    @pl.when(place_ref[0] > 0)
    def _():
        put(ac + bs, bc - as_)

    @pl.when(place_ref[0] == 0)
    def _():
        line = iota((NX, CY), 0)
        real = jnp.where(line <= NX // 2, ac, bc)
        imag = jnp.where(line < NX // 2, -as_, -bs)
        put(real, jnp.where((line == 0) | (line == NX // 2), bc, imag))


def quarter(a, b, c, d, sign):
    def add(p, q):
        return (p[0] + q[0], p[1] + q[1])

    def sub(p, q):
        return (p[0] - q[0], p[1] - q[1])

    first, second, third, fourth = add(a, c), sub(a, c), add(b, d), sub(b, d)
    fourth = (-fourth[1], fourth[0]) if sign > 0 else (fourth[1], -fourth[0])
    return [add(first, third), add(second, fourth), sub(first, third), sub(second, fourth)]


def eighth(parts, sign):
    even = quarter(parts[0], parts[2], parts[4], parts[6], sign)
    odd = quarter(parts[1], parts[3], parts[5], parts[7], sign)
    root = math.sqrt(0.5)
    a, b = odd[1]
    odd[1] = ((a - sign * b) * root, (b + sign * a) * root)
    a, b = odd[2]
    odd[2] = (-sign * b, sign * a)
    a, b = odd[3]
    odd[3] = ((-a - sign * b) * root, (sign * a - b) * root)
    return [(e[0] + o[0], e[1] + o[1]) for e, o in zip(even, odd)] + [
        (e[0] - o[0], e[1] - o[1]) for e, o in zip(even, odd)
    ]


def times(value, table):
    high, low = split(value)
    return dot(high, table[0]) + dot(low, table[0]) + dot(high, table[1])


def line_kernel(place_ref, recv_ref, spec_ref, turn_ref, forward_ref, inverse_ref, send_ref):
    special = place_ref[1]
    top = (iota((8, CY), 0) == 0) & (special > 0)
    parts = []
    for q in range(PENCILS):
        real = recv_ref[q, 0:LINES, :].astype(F32)
        imag = recv_ref[q, LINES : 2 * LINES, :].astype(F32)
        first = imag[0:8]
        real = jnp.concatenate([real, jnp.where(top, first, 0.0)], 0)
        imag = jnp.concatenate(
            [jnp.where(top, 0.0, first), imag[8:], jnp.zeros((8, CY), F32)], 0
        )
        parts.append((real, imag))
    parts = eighth(parts, -1)
    lines = []
    for k in range(PENCILS):
        real, imag = parts[k]
        if k > 0:
            c = turn_ref[k : k + 1, :]
            s = turn_ref[PENCILS + k : PENCILS + k + 1, :]
            real, imag = real * c + imag * s, imag * c - real * s
        lines.append(jnp.concatenate([real, imag], 1))
    wave = times(jnp.concatenate(lines, 0), (forward_ref[0], forward_ref[1]))
    spec = spec_ref[...]
    wave = wave * jnp.concatenate([spec, spec], 1)
    wave = times(wave, (inverse_ref[0], inverse_ref[1]))
    parts = []
    for k in range(PENCILS):
        real = wave[k * MORE : (k + 1) * MORE, :CY]
        imag = wave[k * MORE : (k + 1) * MORE, CY:]
        if k > 0:
            c = turn_ref[k : k + 1, :]
            s = turn_ref[PENCILS + k : PENCILS + k + 1, :]
            real, imag = real * c - imag * s, imag * c + real * s
        parts.append((real, imag))
    parts = eighth(parts, 1)
    for q in range(PENCILS):
        real, imag = parts[q]
        send_ref[q] = jnp.concatenate(
            [
                real[0:8] - imag[LINES:],
                real[8:LINES],
                imag[0:8] + real[LINES:],
                imag[8:LINES],
            ],
            0,
        ).astype(BF16)


def sample_kernel(place_ref, pos_ref, recv_ref, table_ref, send_hbm, left_ref, wave_ref, send_ref, sems):
    real = jnp.concatenate([recv_ref[r, 0:LINES, :] for r in range(PENCILS)], 0)
    imag = jnp.concatenate([recv_ref[r, LINES : 2 * LINES, :] for r in range(PENCILS)], 0)
    real = real.astype(F32).T
    imag = imag.astype(F32).T

    def put(first, second, third, fourth):
        wave_ref[0:CY, 0:NX] = first.astype(BF16)
        wave_ref[0:CY, NX:] = second.astype(BF16)
        wave_ref[CY:, 0:NX] = third.astype(BF16)
        wave_ref[CY:, NX:] = fourth.astype(BF16)

    @pl.when(place_ref[0] > 0)
    def _():
        put(real, -imag, imag, real)

    @pl.when(place_ref[0] == 0)
    def _():
        line = iota((CY, NX), 1)
        ends = (line == 0) | (line == NX // 2)
        low = line < NX // 2
        put(
            jnp.where(ends, real, jnp.where(low, 2.0 * real, 0.0)),
            jnp.where(ends, 0.0, jnp.where(low, -2.0 * imag, 0.0)),
            jnp.where(ends, imag, jnp.where(low, 0.0, 2.0 * real)),
            jnp.where(ends, 0.0, jnp.where(low, 0.0, -2.0 * imag)),
        )

    plane = dot(wave_ref[...], table_ref[...])
    for half in range(2):
        part = plane[:, half * SPAN : (half + 1) * SPAN]
        for i in range(4):
            moved = part if i == 0 else pltpu.roll(part, SPAN - WINDOW * i, 1)
            left_ref[half, 2 * CY * i : 2 * CY * (i + 1), :] = moved[:, :TILE].astype(BF16)

    cells = iota((TILE, 128), 0).astype(F32)
    y_cells = (iota((16, 8, 128), 0) * 8 + iota((16, 8, 128), 1)).astype(F32)
    upper = iota((8, 128), 0) < 4

    def gather(step):
        quads = [step * 2, step * 2 + 1]
        found = {}
        for half in range(2):
            hot, inside = [], []
            for quad in quads:
                place = pos_ref[quad]
                code, y_place = place[2 * half : 2 * half + 1], place[2 * half + 1 : 2 * half + 2]
                hot.append(jnp.where(cells == code, 1.0, 0.0).astype(BF16))
                away = y_cells - y_place[None]
                inside.append((away >= 0.0) & (away < 4.0))
            hot = jnp.concatenate(hot, 1)
            for i in range(4):
                part = dot(left_ref[half, 2 * CY * i : 2 * CY * (i + 1), :], hot)
                for near in range(2):
                    for c in range(2):
                        block = part[c * CY : (c + 1) * CY, near * 128 : (near + 1) * 128]
                        block = jnp.where(inside[near], block.reshape(16, 8, 128), 0.0)
                        block = jnp.sum(block, axis=0)
                        found[near, c, half, i] = block + pltpu.roll(block, 4, 0)
        for near in range(2):
            tiles = []
            for c in range(2):
                for half in range(2):
                    f = [found[near, c, half, i] for i in range(4)]
                    tiles.append(
                        jnp.concatenate(
                            [jnp.where(upper, f[0], f[1]), jnp.where(upper, f[2], f[3])], 0
                        )
                    )
            for n, tile in enumerate(ungroup(tiles)):
                send_ref[quads[near] * 4 + n] = tile.astype(BF16)

    copies = []
    for step in range(SLABS // 8):
        gather(step)
        rows = slice(step * 8, (step + 1) * 8)
        copies.append(pltpu.make_async_copy(send_ref.at[rows], send_hbm.at[rows], sems.at[step]))
        copies[-1].start()
    for copy in copies:
        copy.wait()


def finish_kernel(
    phase_ref, side_hbm, recv_ref, proj_ref, out_ref, value_ref, wide_ref, side_ref, sem
):
    copy = pltpu.make_async_copy(side_hbm, side_ref, sem)
    copy.start()
    totals = [jnp.zeros((16, 128), F32) for _ in range(4)]
    for wave in range(SLABS):
        value = recv_ref[wave].astype(F32)
        for k in range(4):
            totals[k] = totals[k] + phase_ref[k * SLABS + wave : k * SLABS + wave + 1, :] * value
    turn = phase_ref[4 * SLABS : 4 * SLABS + 1, :].astype(jnp.int32) & 3
    row = iota((16, 128), 0) & 3
    for k in range(4):
        value = totals[k] + pltpu.roll(totals[k], BOX, 1)
        out = value
        for m in range(1, 4):
            moved = jnp.where(
                row + m < 4, pltpu.roll(value, 16 - m, 0), pltpu.roll(value, 4 - m, 0)
            )
            out = jnp.where(turn == m, moved, out)
        value_ref[pl.ds(k, 16, stride=4), :] = out
    copy.wait()
    value = dot(value_ref[...].astype(BF16), side_ref[BOX:].astype(BF16))
    value = jnp.concatenate([value, value], 0).T[0:BOX]
    box = iota((BOX, 128), 0)
    half = (iota((BOX, 128), 1) >= STENCIL).astype(jnp.int32)
    for m in range(BOX // 2):
        wide_ref[:, 128 * m : 128 * (m + 1)] = jnp.where(
            box == 2 * m + half, value, 0.0
        ).astype(BF16)
    out_ref[...] = dot(wide_ref[...], proj_ref[...]) + side_ref[0:BOX]


def near_kernel(ids_ref, small_ref, group_ref, near_ref, phase_ref, side_hbm, side_ref, sem):
    phases(small_ref[1:2, :].astype(jnp.int32), phase_ref)
    phase_ref[4 * SLABS :] = small_ref[0:8]
    side_ref[BOX:] = small_ref[8:]
    hot = jnp.where(iota((BOX, GROUP), 1) == ids_ref[...], 1.0, 0.0).astype(BF16)
    partner = dot(hot, group_ref[...]).astype(BF16)
    twice = jnp.concatenate([partner, partner], 0)
    lane = iota((FUNCS, 128), 1) & (BOX - 1)

    def step(index, total):
        start = pl.multiple_of(index * 512, 512)
        part = dot(near_ref[pl.ds(start, 512), :], twice, NT)
        for t in range(4):
            total = jnp.where(lane == index * 4 + t, part[t * FUNCS : (t + 1) * FUNCS], total)
        return total

    total = lax.fori_loop(0, BOX // 4, step, jnp.zeros((FUNCS, 128), F32))
    side_ref[0:BOX] = total.T[0:BOX]
    copy = pltpu.make_async_copy(side_ref, side_hbm, sem)
    copy.start()
    copy.wait()


VMEM = pl.BlockSpec(memory_space=pltpu.VMEM)
SMEM = pl.BlockSpec(memory_space=pltpu.SMEM)
HBM = pl.BlockSpec(memory_space=pltpu.HBM)


def call(kernel, shapes, specs, scratch=(), outs=None, limit=32, flops=0, moved=0):
    return pl.pallas_call(
        kernel,
        out_shape=shapes,
        in_specs=specs,
        out_specs=outs or jax.tree.map(lambda _: VMEM, shapes),
        scratch_shapes=list(scratch),
        compiler_params=pltpu.CompilerParams(vmem_limit_bytes=limit * 1024 * 1024),
        cost_estimate=pl.CostEstimate(flops=flops, bytes_accessed=moved, transcendentals=0),
    )


def resident(*arrays, space=pltpu.HBM):
    return [pltpu.with_memory_space_constraint(a, space) for a in arrays]


def struct(*shape, kind=F32):
    return jax.ShapeDtypeStruct(shape, kind)


def project(anchors, slabs, coefficients, flat):
    return call(
        project_kernel,
        (
            pltpu.HBM((SLABS, ROWS // 2, 2, 128), BF16),
            pltpu.HBM((SMALL, 128), F32),
        ),
        [HBM] * 4,
        [
            pltpu.VMEM((SLABS, ROWS // 2, 2, 128), BF16),
            pltpu.VMEM((SMALL, 128), F32),
            pltpu.VMEM((4 * SLABS, 128), F32),
            pltpu.VMEM((STENCIL, 128), F32),
            pltpu.VMEM(anchors.shape, jnp.int32),
            pltpu.VMEM(slabs.shape, jnp.int32),
            pltpu.VMEM(coefficients.shape, BF16),
            pltpu.VMEM(flat.shape, BF16),
            pltpu.SemaphoreType.DMA((12,)),
        ],
        outs=(HBM, HBM),
        limit=8,
        flops=2 * BOXES * FUNCS * 128,
        moved=2 << 20,
    )(*resident(anchors, slabs, coefficients, flat))


def spread(place, received, table):
    return call(
        spread_kernel,
        (struct(PENCILS, 2 * LINES, CY, kind=BF16), struct(SLABS // 4, 8, 128)),
        [SMEM] + [VMEM] * 2,
        [pltpu.VMEM((8 * CY, BOXES), BF16), pltpu.VMEM((TILE, BOXES), BF16)],
        limit=28,
        flops=2 * BOXES * TILE * 8 * CY,
        moved=4 << 20,
    )(place, received, table)


def lines(place, received, spec, turn, forward, inverse):
    return call(
        line_kernel,
        struct(PENCILS, 2 * LINES, CY, kind=BF16),
        [SMEM] + [VMEM] * 5,
        limit=12,
        flops=2 * 6 * PENCILS * MORE * 256 * 256,
        moved=2 << 20,
    )(place, received, spec, turn, forward, inverse)


def sample(place, pos, received, table):
    return call(
        sample_kernel,
        pltpu.HBM((SLABS, 16, 128), BF16),
        [SMEM] + [VMEM] * 3,
        [
            pltpu.VMEM((2, 8 * CY, TILE), BF16),
            pltpu.VMEM((2 * CY, 2 * NX), BF16),
            pltpu.VMEM((SLABS, 16, 128), BF16),
            pltpu.SemaphoreType.DMA((SLABS // 8,)),
        ],
        outs=HBM,
        limit=16,
        flops=2 * BOXES * TILE * 8 * CY,
        moved=4 << 20,
    )(place, pos, received, table)


def finish(phase, side, received, flat):
    return call(
        finish_kernel,
        struct(BOX, FUNCS),
        [VMEM, HBM, VMEM, VMEM],
        [
            pltpu.VMEM((STENCIL, 128), F32),
            pltpu.VMEM((BOX, BOX * STENCIL), BF16),
            pltpu.VMEM((SIDE, 128), F32),
            pltpu.SemaphoreType.DMA,
        ],
        limit=8,
        flops=2 * BOX * BOXES * FUNCS,
        moved=2 << 20,
    )(*resident(phase, space=pltpu.VMEM), *resident(side), received, flat)


def near(ids, small, group, blocks):
    return call(
        near_kernel,
        (pltpu.VMEM((4 * SLABS + 8, 128), F32), pltpu.HBM((SIDE, 128), F32)),
        [VMEM] * 4,
        [pltpu.VMEM((SIDE, 128), F32), pltpu.SemaphoreType.DMA],
        outs=(VMEM, HBM),
        limit=8,
        flops=2 * BOX * FUNCS * FUNCS * 128,
        moved=3 << 20,
    )(ids, small, group, blocks)


def arrange(spectrum, slab, pencil):
    first, second = spectrum[:, 0, :], spectrum[:, 1, :]
    chosen = jnp.where((slab == 0) & (pencil >= PENCILS // 2), second, first)
    head = jnp.where((slab == 0) & (pencil == PENCILS // 2), first[0:1], chosen[0:1])
    rows = jnp.concatenate([head, chosen[1:], jnp.broadcast_to(second[0:1], (8, NY))], 0)
    rows = rows * jnp.where(slab == 0, 1.0, 2.0) * (1.0 / (NX * NY * NZ))
    return rows.reshape(MORE, CY, PENCILS).transpose(2, 0, 1).reshape(PENCILS * MORE, CY)


def per_device(coefficients, projection, near_blocks, near_ids, grid_slab, anchors, spectrum):
    slab = lax.axis_index("slab")
    pencil = lax.axis_index("pencil")
    special = (slab == 0) & (pencil % (PENCILS // 2) == 0)
    place = jnp.stack([slab, special.astype(jnp.int32)]).astype(jnp.int32)
    flat = projection.reshape(BOX * STENCIL, FUNCS)
    table = jnp.asarray(x_table().astype(BF16))
    forward, inverse, turn = y_tables()
    forward, inverse = np.stack(halves(forward)), np.stack(halves(inverse))

    send, small = project(anchors, grid_slab.reshape(1, BOX), coefficients, flat)
    received = lax.all_to_all(send, "slab", split_axis=0, concat_axis=0, tiled=True)
    spec = arrange(spectrum, slab, pencil)
    received, spec, place = lax.optimization_barrier((received, spec, place))
    send, pos = spread(place, received, table)
    received = lax.all_to_all(send, "pencil", split_axis=0, concat_axis=0, tiled=True)
    send = lines(place, received, spec, turn, forward, inverse)
    received = lax.all_to_all(send, "pencil", split_axis=0, concat_axis=0, tiled=True)
    send = sample(place, pos, received, table)
    send, own = lax.optimization_barrier((send, coefficients))
    received = lax.all_to_all(send, "slab", split_axis=0, concat_axis=0, tiled=True)
    group = lax.all_gather(own, "pencil", axis=0, tiled=True)
    blocks = near_blocks.reshape(BOX * FUNCS, FUNCS)
    phase, side = near(near_ids & (GROUP - 1), small, group, blocks)
    return finish(phase, side, received, flat)


def solution(mesh):
    placed = (
        P(("slab", "pencil"), None),
        P(("slab", "pencil"), None, None),
        P(("slab", "pencil"), None, None, None),
        P(("slab", "pencil"), None),
        P(("slab", "pencil"), None),
        P(None, ("slab", "pencil")),
        P("pencil", "slab", None),
    )
    return jax.shard_map(
        per_device,
        mesh=mesh,
        in_specs=placed,
        out_specs=P(("slab", "pencil"), None),
        check_vma=False,
    )
```

```python
import math

import jax
import jax.numpy as jnp
import numpy as np
from jax import lax
from jax.experimental import pallas as pl
from jax.experimental.pallas import tpu as pltpu
from jax.sharding import PartitionSpec as P

SLABS = 64
PENCILS = 8
BOX = 64
FUNCS = 128
STENCIL = 64
CX = 8
CY = 128
NX = 512
NY = 1024
NZ = 128
GROUP = BOX * PENCILS
ROWS = 18
LINES = NX // PENCILS
MORE = LINES + 8
BOXES = SLABS * BOX
SMALL = 8 + 128
SIDE = BOX + 128
TILE = 256
WINDOW = 48
SHIFT = SLABS - WINDOW
SPAN = CX * WINDOW

F32 = jnp.float32
BF16 = jnp.bfloat16
NT = (((1,), (1,)), ((), ()))
NN = (((1,), (0,)), ((), ()))


def halves(table):
    table = np.asarray(table, np.float32)
    high = table.astype(BF16)
    low = (table - high.astype(np.float32)).astype(BF16)
    return high, low


def x_table():
    half, offset, slab = np.meshgrid(
        np.arange(2), np.arange(CX), np.arange(WINDOW), indexing="ij"
    )
    cells = (CX * (slab + SHIFT * half) + offset).reshape(-1)
    phase = np.outer(np.arange(NX), cells) % NX * (2.0 * math.pi / NX)
    return np.concatenate([np.cos(phase), np.sin(phase)], 0)


def y_tables():
    phase = np.outer(np.arange(CY), np.arange(CY)) % CY * (2.0 * math.pi / CY)
    c, s = np.cos(phase), np.sin(phase)
    forward = np.block([[c, -s], [s, c]])
    inverse = np.block([[c, s], [-s, c]])
    turn = np.outer(np.arange(PENCILS), np.arange(CY)) * (2.0 * math.pi / NY)
    turn = np.concatenate([np.cos(turn), np.sin(turn)], 0).astype(np.float32)
    return forward, inverse, turn


def cosine_coefficients():
    fit = np.polynomial.chebyshev.Chebyshev.interpolate(
        lambda w: np.cos(2.0 * math.pi * np.sqrt(w)), 9, domain=[0.0, 0.25]
    )
    return [float(v) for v in fit.convert(kind=np.polynomial.Polynomial).coef]


COSINE = cosine_coefficients()


def cosine_of(step):
    u = (step.astype(F32) - (NZ // 2)) * (1.0 / NZ)
    w = u * u
    total = jnp.full_like(w, COSINE[-1])
    for value in COSINE[-2::-1]:
        total = total * w + value
    return -total


def iota(shape, axis):
    return lax.broadcasted_iota(jnp.int32, shape, axis)


def dot(a, b, dims=NN):
    return lax.dot_general(a, b, dims, preferred_element_type=F32)


def split(value):
    high = value.astype(BF16)
    return high, (value - high.astype(F32)).astype(BF16)


def swap(first, other, width):
    even = iota(first.shape, 1) & width == 0
    return (
        jnp.where(even, first, pltpu.roll(other, width, 1)),
        jnp.where(even, pltpu.roll(first, 128 - width, 1), other),
    )


def regroup(tiles):
    a, c = swap(tiles[0], tiles[2], 64)
    b, d = swap(tiles[1], tiles[3], 64)
    return swap(a, b, 32) + swap(c, d, 32)


def ungroup(tiles):
    a, b = swap(tiles[0], tiles[1], 32)
    c, d = swap(tiles[2], tiles[3], 32)
    first, third = swap(a, c, 64)
    second, fourth = swap(b, d, 64)
    return first, second, third, fourth


def phases(depth, phase_ref):
    second = (iota((SLABS, 128), 1) >= BOX).astype(jnp.int32)
    wave = iota((SLABS, 128), 0)
    for k in range(4):
        z = depth + k
        step = jnp.where(wave == 0, second * (NZ // 2) * z, wave * z + second * (NZ // 4))
        phase_ref[k * SLABS : (k + 1) * SLABS] = cosine_of(step & (NZ - 1))


def project_kernel(
    anchor_hbm, slab_hbm, coef_hbm, proj_hbm,
    send_hbm, small_hbm,
    send_ref, small_ref, phase_ref, value_ref, anchor_ref, slab_ref, coef_ref, proj_ref, sems,
):
    small = [
        pltpu.make_async_copy(source, target, sems.at[n])
        for n, (source, target) in enumerate(
            ((slab_hbm, slab_ref), (anchor_hbm, anchor_ref), (coef_hbm, coef_ref))
        )
    ]
    for copy in small:
        copy.start()
    large = pltpu.make_async_copy(proj_hbm, proj_ref, sems.at[3])
    large.start()
    for copy in small:
        copy.wait()

    slab = slab_ref[...].astype(F32)
    box = iota((1, BOX), 1).astype(F32)
    key = slab * BOX + box
    key = jnp.concatenate([key, key], 1)
    column = jnp.broadcast_to(key, (128, 128)).T[0:BOX]
    rank = jnp.sum(jnp.where(column < key, 1.0, 0.0), axis=0, keepdims=True)
    column = jnp.broadcast_to(rank, (128, 128)).T[0:BOX]
    lane = (iota((BOX, 128), 1) & (BOX - 1)).astype(F32)
    chosen = column == lane
    order = jnp.sum(
        jnp.where(chosen, iota((BOX, 128), 0).astype(F32), 0.0), axis=0, keepdims=True
    )
    row = iota((128, 128), 0)
    hot = jnp.where((row & (BOX - 1)).astype(F32) == rank, 1.0, 0.0)
    twice = dot(hot.astype(BF16)[:, 0:BOX], coef_ref[...]).astype(BF16)
    table = jnp.concatenate(
        [anchor_ref[...].astype(F32), slab, jnp.zeros((4, BOX), F32)], 0
    ).astype(BF16)
    table = dot(table, jnp.where(chosen, 1.0, 0.0).astype(BF16))
    later = (iota((1, 128), 1) & (BOX // 2) > 0).astype(F32)
    code = table[0:1] * WINDOW + table[3:4] - later * SHIFT
    y_place = table[1:2]
    depth = table[2:3].astype(jnp.int32)
    small_ref[0:8] = jnp.concatenate([y_place, table[2:3], jnp.zeros((6, 128), F32)], 0)
    small_ref[8:] = jnp.where(row < BOX, hot, 0.0)
    notes = pltpu.make_async_copy(small_ref, small_hbm, sems.at[8])
    notes.start()
    phases(depth, phase_ref)

    large.wait()
    every = dot(proj_ref[...], twice, NT)
    total = jnp.zeros((STENCIL, 128), F32)
    for n in range(BOX):
        part = every[n * STENCIL : (n + 1) * STENCIL]
        total = jnp.where(order == float(n), part, total)
    value_ref[...] = total

    turn = y_place.astype(jnp.int32) & 3
    row = iota((16, 128), 0) & 3
    parts = []
    for k in range(4):
        value = value_ref[pl.ds(k, 16, stride=4), :]
        out = value
        for m in range(1, 4):
            moved = jnp.where(row >= m, pltpu.roll(value, m, 0), pltpu.roll(value, m + 12, 0))
            out = jnp.where(turn == m, moved, out)
        parts.append(out)
    places = jnp.where(iota((8, 128), 1) < BOX, code, y_place)[0 : ROWS - 16]
    size = SLABS // 4
    copies = []
    for wave in range(SLABS):
        total = phase_ref[wave : wave + 1, :] * parts[0]
        for k in range(1, 4):
            row = k * SLABS + wave
            total = total + phase_ref[row : row + 1, :] * parts[k]
        total = jnp.concatenate([total, places], 0).reshape(ROWS // 2, 2, 128)
        send_ref[wave] = total.astype(BF16)
        if wave % size == size - 1:
            n = wave // size
            copies.append(
                pltpu.make_async_copy(
                    send_ref.at[n * size : (n + 1) * size],
                    send_hbm.at[n * size : (n + 1) * size],
                    sems.at[4 + n],
                )
            )
            copies[-1].start()
    for copy in copies:
        copy.wait()
    notes.wait()


def spread_kernel(place_ref, recv_ref, table_ref, send_ref, pos_ref, row_ref, hot_ref):
    cells = iota((TILE, 128), 0).astype(F32)
    y_cells = iota((CY, 128), 0).astype(F32)
    upper = iota((8, 128), 0) < 4

    groups = []
    for step in range(SLABS // 4):
        tiles = []
        for n in range(4):
            tile = recv_ref[step * 4 + n].astype(F32).reshape(ROWS, 128)
            tiles.append(jnp.concatenate([tile, jnp.zeros((24 - ROWS, 128), F32)], 0))
        tiles = regroup(tiles)
        groups.append(((tiles[0], tiles[2]), (tiles[1], tiles[3])))
        places = [tile[16:17] for pair in groups[-1] for tile in pair]
        pos_ref[step] = jnp.concatenate(places + [jnp.zeros((4, 128), F32)], 0)

    def fill(step, half):
        real, imag = groups[step][half]
        code, y_place = real[16:17], imag[16:17]
        start = half * (BOXES // 2) + step * 128
        away = y_cells - y_place
        inside = jnp.where((away >= 0.0) & (away < 4.0), 1.0, 0.0).astype(BF16)
        inside = inside.reshape(8, 16, 128)
        for i in range(4):
            for c, source in enumerate((real, imag)):
                block = source[8 * (i // 2) : 8 * (i // 2) + 8]
                moved = pltpu.roll(block, 4, 0)
                pair = (block, moved) if i % 2 == 0 else (moved, block)
                both = jnp.where(upper, pair[0], pair[1])
                both = jnp.concatenate([both, both], 0).astype(BF16)
                rows = (inside * both[None]).reshape(CY, 128)
                row_ref[(2 * i + c) * CY : (2 * i + c + 1) * CY, start : start + 128] = rows
        hot_ref[:, start : start + 128] = jnp.where(cells == code, 1.0, 0.0).astype(BF16)

    count = 4
    steps = SLABS // 4 // count
    size = BOXES // 2 // count
    parts = [[None] * 4 for _ in range(2)]
    for run in range(count):
        for half in range(2):
            for step in range(run * steps, (run + 1) * steps):
                fill(step, half)
            start = half * (BOXES // 2) + run * size
            lanes = slice(start, start + size)
            for i in range(4):
                part = dot(row_ref[2 * CY * i : 2 * CY * (i + 1), lanes], hot_ref[:, lanes], NT)
                parts[half][i] = part if run == 0 else parts[half][i] + part
    planes = []
    for half in range(2):
        plane = None
        for i in range(4):
            part = jnp.concatenate([parts[half][i], jnp.zeros((2 * CY, SPAN - TILE), F32)], 1)
            plane = part if i == 0 else plane + pltpu.roll(part, WINDOW * i, 1)
        planes.append(plane)
    wave = dot(table_ref[...], jnp.concatenate(planes, 1).astype(BF16), NT)
    ac, bc = wave[:NX, :CY], wave[:NX, CY:]
    as_, bs = wave[NX:, :CY], wave[NX:, CY:]

    def put(real, imag):
        real = real.astype(BF16)
        imag = imag.astype(BF16)
        for r in range(PENCILS):
            send_ref[r, 0:LINES, :] = real[r * LINES : (r + 1) * LINES]
            send_ref[r, LINES : 2 * LINES, :] = imag[r * LINES : (r + 1) * LINES]

    @pl.when(place_ref[0] > 0)
    def _():
        put(ac + bs, bc - as_)

    @pl.when(place_ref[0] == 0)
    def _():
        line = iota((NX, CY), 0)
        real = jnp.where(line <= NX // 2, ac, bc)
        imag = jnp.where(line < NX // 2, -as_, -bs)
        put(real, jnp.where((line == 0) | (line == NX // 2), bc, imag))


def quarter(a, b, c, d, sign):
    def add(p, q):
        return (p[0] + q[0], p[1] + q[1])

    def sub(p, q):
        return (p[0] - q[0], p[1] - q[1])

    first, second, third, fourth = add(a, c), sub(a, c), add(b, d), sub(b, d)
    fourth = (-fourth[1], fourth[0]) if sign > 0 else (fourth[1], -fourth[0])
    return [add(first, third), add(second, fourth), sub(first, third), sub(second, fourth)]


def eighth(parts, sign):
    even = quarter(parts[0], parts[2], parts[4], parts[6], sign)
    odd = quarter(parts[1], parts[3], parts[5], parts[7], sign)
    root = math.sqrt(0.5)
    a, b = odd[1]
    odd[1] = ((a - sign * b) * root, (b + sign * a) * root)
    a, b = odd[2]
    odd[2] = (-sign * b, sign * a)
    a, b = odd[3]
    odd[3] = ((-a - sign * b) * root, (sign * a - b) * root)
    return [(e[0] + o[0], e[1] + o[1]) for e, o in zip(even, odd)] + [
        (e[0] - o[0], e[1] - o[1]) for e, o in zip(even, odd)
    ]


def times(value, table):
    high, low = split(value)
    return dot(high, table[0]) + dot(low, table[0]) + dot(high, table[1])


def line_kernel(place_ref, recv_ref, spec_ref, turn_ref, forward_ref, inverse_ref, send_ref):
    special = place_ref[1]
    top = (iota((8, CY), 0) == 0) & (special > 0)
    parts = []
    for q in range(PENCILS):
        real = recv_ref[q, 0:LINES, :].astype(F32)
        imag = recv_ref[q, LINES : 2 * LINES, :].astype(F32)
        first = imag[0:8]
        real = jnp.concatenate([real, jnp.where(top, first, 0.0)], 0)
        imag = jnp.concatenate(
            [jnp.where(top, 0.0, first), imag[8:], jnp.zeros((8, CY), F32)], 0
        )
        parts.append((real, imag))
    parts = eighth(parts, -1)
    lines = []
    for k in range(PENCILS):
        real, imag = parts[k]
        if k > 0:
            c = turn_ref[k : k + 1, :]
            s = turn_ref[PENCILS + k : PENCILS + k + 1, :]
            real, imag = real * c + imag * s, imag * c - real * s
        lines.append(jnp.concatenate([real, imag], 1))
    wave = times(jnp.concatenate(lines, 0), (forward_ref[0], forward_ref[1]))
    spec = spec_ref[...]
    wave = wave * jnp.concatenate([spec, spec], 1)
    wave = times(wave, (inverse_ref[0], inverse_ref[1]))
    parts = []
    for k in range(PENCILS):
        real = wave[k * MORE : (k + 1) * MORE, :CY]
        imag = wave[k * MORE : (k + 1) * MORE, CY:]
        if k > 0:
            c = turn_ref[k : k + 1, :]
            s = turn_ref[PENCILS + k : PENCILS + k + 1, :]
            real, imag = real * c - imag * s, imag * c + real * s
        parts.append((real, imag))
    parts = eighth(parts, 1)
    for q in range(PENCILS):
        real, imag = parts[q]
        send_ref[q] = jnp.concatenate(
            [
                real[0:8] - imag[LINES:],
                real[8:LINES],
                imag[0:8] + real[LINES:],
                imag[8:LINES],
            ],
            0,
        ).astype(BF16)


def sample_kernel(place_ref, pos_ref, recv_ref, table_ref, send_hbm, left_ref, wave_ref, send_ref, sems):
    real = jnp.concatenate([recv_ref[r, 0:LINES, :] for r in range(PENCILS)], 0)
    imag = jnp.concatenate([recv_ref[r, LINES : 2 * LINES, :] for r in range(PENCILS)], 0)
    real = real.astype(F32).T
    imag = imag.astype(F32).T

    def put(first, second, third, fourth):
        wave_ref[0:CY, 0:NX] = first.astype(BF16)
        wave_ref[0:CY, NX:] = second.astype(BF16)
        wave_ref[CY:, 0:NX] = third.astype(BF16)
        wave_ref[CY:, NX:] = fourth.astype(BF16)

    @pl.when(place_ref[0] > 0)
    def _():
        put(real, -imag, imag, real)

    @pl.when(place_ref[0] == 0)
    def _():
        line = iota((CY, NX), 1)
        ends = (line == 0) | (line == NX // 2)
        low = line < NX // 2
        put(
            jnp.where(ends, real, jnp.where(low, 2.0 * real, 0.0)),
            jnp.where(ends, 0.0, jnp.where(low, -2.0 * imag, 0.0)),
            jnp.where(ends, imag, jnp.where(low, 0.0, 2.0 * real)),
            jnp.where(ends, 0.0, jnp.where(low, 0.0, -2.0 * imag)),
        )

    plane = dot(wave_ref[...], table_ref[...])
    for half in range(2):
        part = plane[:, half * SPAN : (half + 1) * SPAN]
        for i in range(4):
            moved = part if i == 0 else pltpu.roll(part, SPAN - WINDOW * i, 1)
            left_ref[half, 2 * CY * i : 2 * CY * (i + 1), :] = moved[:, :TILE].astype(BF16)

    cells = iota((TILE, 128), 0).astype(F32)
    y_cells = (iota((16, 8, 128), 0) * 8 + iota((16, 8, 128), 1)).astype(F32)
    upper = iota((8, 128), 0) < 4

    def gather(step):
        quads = [step * 2, step * 2 + 1]
        found = {}
        for half in range(2):
            hot, inside = [], []
            for quad in quads:
                place = pos_ref[quad]
                code, y_place = place[2 * half : 2 * half + 1], place[2 * half + 1 : 2 * half + 2]
                hot.append(jnp.where(cells == code, 1.0, 0.0).astype(BF16))
                away = y_cells - y_place[None]
                inside.append((away >= 0.0) & (away < 4.0))
            hot = jnp.concatenate(hot, 1)
            for i in range(4):
                part = dot(left_ref[half, 2 * CY * i : 2 * CY * (i + 1), :], hot)
                for near in range(2):
                    for c in range(2):
                        block = part[c * CY : (c + 1) * CY, near * 128 : (near + 1) * 128]
                        block = jnp.where(inside[near], block.reshape(16, 8, 128), 0.0)
                        block = jnp.sum(block, axis=0)
                        found[near, c, half, i] = block + pltpu.roll(block, 4, 0)
        for near in range(2):
            tiles = []
            for c in range(2):
                for half in range(2):
                    f = [found[near, c, half, i] for i in range(4)]
                    tiles.append(
                        jnp.concatenate(
                            [jnp.where(upper, f[0], f[1]), jnp.where(upper, f[2], f[3])], 0
                        )
                    )
            for n, tile in enumerate(ungroup(tiles)):
                send_ref[quads[near] * 4 + n] = tile.astype(BF16)

    copies = []
    for step in range(SLABS // 8):
        gather(step)
        rows = slice(step * 8, (step + 1) * 8)
        copies.append(pltpu.make_async_copy(send_ref.at[rows], send_hbm.at[rows], sems.at[step]))
        copies[-1].start()
    for copy in copies:
        copy.wait()


def finish_kernel(
    phase_ref, side_hbm, recv_ref, proj_ref, out_ref, value_ref, wide_ref, side_ref, sem
):
    copy = pltpu.make_async_copy(side_hbm, side_ref, sem)
    copy.start()
    totals = [jnp.zeros((16, 128), F32) for _ in range(4)]
    for wave in range(SLABS):
        value = recv_ref[wave].astype(F32)
        for k in range(4):
            totals[k] = totals[k] + phase_ref[k * SLABS + wave : k * SLABS + wave + 1, :] * value
    turn = phase_ref[4 * SLABS : 4 * SLABS + 1, :].astype(jnp.int32) & 3
    row = iota((16, 128), 0) & 3
    for k in range(4):
        value = totals[k] + pltpu.roll(totals[k], BOX, 1)
        out = value
        for m in range(1, 4):
            moved = jnp.where(
                row + m < 4, pltpu.roll(value, 16 - m, 0), pltpu.roll(value, 4 - m, 0)
            )
            out = jnp.where(turn == m, moved, out)
        value_ref[pl.ds(k, 16, stride=4), :] = out
    copy.wait()
    value = dot(value_ref[...].astype(BF16), side_ref[BOX:].astype(BF16))
    value = jnp.concatenate([value, value], 0).T[0:BOX]
    box = iota((BOX, 128), 0)
    half = (iota((BOX, 128), 1) >= STENCIL).astype(jnp.int32)
    for m in range(BOX // 2):
        wide_ref[:, 128 * m : 128 * (m + 1)] = jnp.where(
            box == 2 * m + half, value, 0.0
        ).astype(BF16)
    out_ref[...] = dot(wide_ref[...], proj_ref[...]) + side_ref[0:BOX]


def near_kernel(ids_ref, small_ref, group_ref, near_ref, phase_ref, side_hbm, side_ref, sem):
    phases(small_ref[1:2, :].astype(jnp.int32), phase_ref)
    phase_ref[4 * SLABS :] = small_ref[0:8]
    side_ref[BOX:] = small_ref[8:]
    hot = jnp.where(iota((BOX, GROUP), 1) == ids_ref[...], 1.0, 0.0).astype(BF16)
    partner = dot(hot, group_ref[...]).astype(BF16)
    twice = jnp.concatenate([partner, partner], 0)
    lane = iota((FUNCS, 128), 1) & (BOX - 1)

    def step(index, total):
        start = pl.multiple_of(index * 512, 512)
        part = dot(near_ref[pl.ds(start, 512), :], twice, NT)
        for t in range(4):
            total = jnp.where(lane == index * 4 + t, part[t * FUNCS : (t + 1) * FUNCS], total)
        return total

    total = lax.fori_loop(0, BOX // 4, step, jnp.zeros((FUNCS, 128), F32))
    side_ref[0:BOX] = total.T[0:BOX]
    copy = pltpu.make_async_copy(side_ref, side_hbm, sem)
    copy.start()
    copy.wait()


VMEM = pl.BlockSpec(memory_space=pltpu.VMEM)
SMEM = pl.BlockSpec(memory_space=pltpu.SMEM)
HBM = pl.BlockSpec(memory_space=pltpu.HBM)


def call(kernel, shapes, specs, scratch=(), outs=None, limit=32, flops=0, moved=0):
    return pl.pallas_call(
        kernel,
        out_shape=shapes,
        in_specs=specs,
        out_specs=outs or jax.tree.map(lambda _: VMEM, shapes),
        scratch_shapes=list(scratch),
        compiler_params=pltpu.CompilerParams(vmem_limit_bytes=limit * 1024 * 1024),
        cost_estimate=pl.CostEstimate(flops=flops, bytes_accessed=moved, transcendentals=0),
    )


def resident(*arrays, space=pltpu.HBM):
    return [pltpu.with_memory_space_constraint(a, space) for a in arrays]


def struct(*shape, kind=F32):
    return jax.ShapeDtypeStruct(shape, kind)


def project(anchors, slabs, coefficients, flat):
    return call(
        project_kernel,
        (
            pltpu.HBM((SLABS, ROWS // 2, 2, 128), BF16),
            pltpu.HBM((SMALL, 128), F32),
        ),
        [HBM] * 4,
        [
            pltpu.VMEM((SLABS, ROWS // 2, 2, 128), BF16),
            pltpu.VMEM((SMALL, 128), F32),
            pltpu.VMEM((4 * SLABS, 128), F32),
            pltpu.VMEM((STENCIL, 128), F32),
            pltpu.VMEM(anchors.shape, jnp.int32),
            pltpu.VMEM(slabs.shape, jnp.int32),
            pltpu.VMEM(coefficients.shape, BF16),
            pltpu.VMEM(flat.shape, BF16),
            pltpu.SemaphoreType.DMA((9,)),
        ],
        outs=(HBM, HBM),
        limit=8,
        flops=2 * BOXES * FUNCS * 128,
        moved=2 << 20,
    )(*resident(anchors, slabs, coefficients, flat))


def spread(place, received, table):
    return call(
        spread_kernel,
        (struct(PENCILS, 2 * LINES, CY, kind=BF16), struct(SLABS // 4, 8, 128)),
        [SMEM] + [VMEM] * 2,
        [pltpu.VMEM((8 * CY, BOXES), BF16), pltpu.VMEM((TILE, BOXES), BF16)],
        limit=28,
        flops=2 * BOXES * TILE * 8 * CY,
        moved=4 << 20,
    )(place, received, table)


def lines(place, received, spec, turn, forward, inverse):
    return call(
        line_kernel,
        struct(PENCILS, 2 * LINES, CY, kind=BF16),
        [SMEM] + [VMEM] * 5,
        limit=12,
        flops=2 * 6 * PENCILS * MORE * 256 * 256,
        moved=2 << 20,
    )(place, received, spec, turn, forward, inverse)


def sample(place, pos, received, table):
    return call(
        sample_kernel,
        pltpu.HBM((SLABS, 16, 128), BF16),
        [SMEM] + [VMEM] * 3,
        [
            pltpu.VMEM((2, 8 * CY, TILE), BF16),
            pltpu.VMEM((2 * CY, 2 * NX), BF16),
            pltpu.VMEM((SLABS, 16, 128), BF16),
            pltpu.SemaphoreType.DMA((SLABS // 8,)),
        ],
        outs=HBM,
        limit=16,
        flops=2 * BOXES * TILE * 8 * CY,
        moved=4 << 20,
    )(place, pos, received, table)


def finish(phase, side, received, flat):
    return call(
        finish_kernel,
        struct(BOX, FUNCS),
        [VMEM, HBM, VMEM, VMEM],
        [
            pltpu.VMEM((STENCIL, 128), F32),
            pltpu.VMEM((BOX, BOX * STENCIL), BF16),
            pltpu.VMEM((SIDE, 128), F32),
            pltpu.SemaphoreType.DMA,
        ],
        limit=8,
        flops=2 * BOX * BOXES * FUNCS,
        moved=2 << 20,
    )(*resident(phase, space=pltpu.VMEM), *resident(side), received, flat)


def near(ids, small, group, blocks):
    return call(
        near_kernel,
        (pltpu.VMEM((4 * SLABS + 8, 128), F32), pltpu.HBM((SIDE, 128), F32)),
        [VMEM] * 4,
        [pltpu.VMEM((SIDE, 128), F32), pltpu.SemaphoreType.DMA],
        outs=(VMEM, HBM),
        limit=8,
        flops=2 * BOX * FUNCS * FUNCS * 128,
        moved=3 << 20,
    )(ids, small, group, blocks)


def arrange(spectrum, slab, pencil):
    first, second = spectrum[:, 0, :], spectrum[:, 1, :]
    chosen = jnp.where((slab == 0) & (pencil >= PENCILS // 2), second, first)
    head = jnp.where((slab == 0) & (pencil == PENCILS // 2), first[0:1], chosen[0:1])
    rows = jnp.concatenate([head, chosen[1:], jnp.broadcast_to(second[0:1], (8, NY))], 0)
    rows = rows * jnp.where(slab == 0, 1.0, 2.0) * (1.0 / (NX * NY * NZ))
    return rows.reshape(MORE, CY, PENCILS).transpose(2, 0, 1).reshape(PENCILS * MORE, CY)


def per_device(coefficients, projection, near_blocks, near_ids, grid_slab, anchors, spectrum):
    slab = lax.axis_index("slab")
    pencil = lax.axis_index("pencil")
    special = (slab == 0) & (pencil % (PENCILS // 2) == 0)
    place = jnp.stack([slab, special.astype(jnp.int32)]).astype(jnp.int32)
    flat = projection.reshape(BOX * STENCIL, FUNCS)
    table = jnp.asarray(x_table().astype(BF16))
    forward, inverse, turn = y_tables()
    forward, inverse = np.stack(halves(forward)), np.stack(halves(inverse))

    send, small = project(anchors, grid_slab.reshape(1, BOX), coefficients, flat)
    received = lax.all_to_all(send, "slab", split_axis=0, concat_axis=0, tiled=True)
    spec = arrange(spectrum, slab, pencil)
    received, spec, place = lax.optimization_barrier((received, spec, place))
    send, pos = spread(place, received, table)
    received = lax.all_to_all(send, "pencil", split_axis=0, concat_axis=0, tiled=True)
    send = lines(place, received, spec, turn, forward, inverse)
    received = lax.all_to_all(send, "pencil", split_axis=0, concat_axis=0, tiled=True)
    send = sample(place, pos, received, table)
    send, own = lax.optimization_barrier((send, coefficients))
    received = lax.all_to_all(send, "slab", split_axis=0, concat_axis=0, tiled=True)
    group = lax.all_gather(own, "pencil", axis=0, tiled=True)
    blocks = near_blocks.reshape(BOX * FUNCS, FUNCS)
    phase, side = near(near_ids & (GROUP - 1), small, group, blocks)
    return finish(phase, side, received, flat)


def solution(mesh):
    placed = (
        P(("slab", "pencil"), None),
        P(("slab", "pencil"), None, None),
        P(("slab", "pencil"), None, None, None),
        P(("slab", "pencil"), None),
        P(("slab", "pencil"), None),
        P(None, ("slab", "pencil")),
        P("pencil", "slab", None),
    )
    return jax.shard_map(
        per_device,
        mesh=mesh,
        in_specs=placed,
        out_specs=P(("slab", "pencil"), None),
        check_vma=False,
    )
```

```python
import math

import jax
import jax.numpy as jnp
import numpy as np
from jax import lax
from jax.experimental import pallas as pl
from jax.experimental.pallas import tpu as pltpu
from jax.sharding import PartitionSpec as P

SLABS = 64
PENCILS = 8
BOX = 64
FUNCS = 128
STENCIL = 64
CX = 8
CY = 128
NX = 512
NY = 1024
NZ = 128
GROUP = BOX * PENCILS
ROWS = 18
LINES = NX // PENCILS
MORE = LINES + 8
BOXES = SLABS * BOX
SMALL = 8 + 128
NOTES = 2 * SLABS
ORDER = NOTES + 8
CLOSE = ORDER + BOX
SIDE = CLOSE + BOX
TILE = 256
WINDOW = 48
SHIFT = SLABS - WINDOW
SPAN = CX * WINDOW

F32 = jnp.float32
BF16 = jnp.bfloat16
NT = (((1,), (1,)), ((), ()))
NN = (((1,), (0,)), ((), ()))


def halves(table):
    table = np.asarray(table, np.float32)
    high = table.astype(BF16)
    low = (table - high.astype(np.float32)).astype(BF16)
    return high, low


def x_table():
    half, offset, slab = np.meshgrid(
        np.arange(2), np.arange(CX), np.arange(WINDOW), indexing="ij"
    )
    cells = (CX * (slab + SHIFT * half) + offset).reshape(-1)
    phase = np.outer(np.arange(NX), cells) % NX * (2.0 * math.pi / NX)
    return np.concatenate([np.cos(phase), np.sin(phase)], 0)


def y_tables():
    phase = np.outer(np.arange(CY), np.arange(CY)) % CY * (2.0 * math.pi / CY)
    c, s = np.cos(phase), np.sin(phase)
    forward = np.block([[c, -s], [s, c]])
    inverse = np.block([[c, s], [-s, c]])
    turn = np.outer(np.arange(PENCILS), np.arange(CY)) * (2.0 * math.pi / NY)
    turn = np.concatenate([np.cos(turn), np.sin(turn)], 0).astype(np.float32)
    return forward, inverse, turn


def cosine_coefficients():
    fit = np.polynomial.chebyshev.Chebyshev.interpolate(
        lambda w: np.cos(2.0 * math.pi * np.sqrt(w)), 9, domain=[0.0, 0.25]
    )
    return [float(v) for v in fit.convert(kind=np.polynomial.Polynomial).coef]


COSINE = cosine_coefficients()


def cosine_of(step):
    u = (step.astype(F32) - (NZ // 2)) * (1.0 / NZ)
    w = u * u
    total = jnp.full_like(w, COSINE[-1])
    for value in COSINE[-2::-1]:
        total = total * w + value
    return -total


def iota(shape, axis):
    return lax.broadcasted_iota(jnp.int32, shape, axis)


def dot(a, b, dims=NN):
    return lax.dot_general(a, b, dims, preferred_element_type=F32)


def split(value):
    high = value.astype(BF16)
    return high, (value - high.astype(F32)).astype(BF16)


def swap(first, other, width):
    even = iota(first.shape, 1) & width == 0
    return (
        jnp.where(even, first, pltpu.roll(other, width, 1)),
        jnp.where(even, pltpu.roll(first, 128 - width, 1), other),
    )


def regroup(tiles):
    a, c = swap(tiles[0], tiles[2], 64)
    b, d = swap(tiles[1], tiles[3], 64)
    return swap(a, b, 32) + swap(c, d, 32)


def ungroup(tiles):
    a, b = swap(tiles[0], tiles[1], 32)
    c, d = swap(tiles[2], tiles[3], 32)
    first, third = swap(a, c, 64)
    second, fourth = swap(b, d, 64)
    return first, second, third, fourth


def phases(depth, phase_ref, count):
    second = (iota((SLABS, 128), 1) >= BOX).astype(jnp.int32)
    wave = iota((SLABS, 128), 0)
    for k in range(count):
        z = depth + k
        step = jnp.where(wave == 0, second * (NZ // 2) * z, wave * z + second * (NZ // 4))
        phase_ref[k * SLABS : (k + 1) * SLABS] = cosine_of(step & (NZ - 1))


def project_kernel(
    anchor_hbm, slab_hbm, coef_hbm, proj_hbm,
    send_hbm, small_hbm,
    send_ref, small_ref, phase_ref, value_ref, anchor_ref, slab_ref, coef_ref, proj_ref, sems,
):
    small = [
        pltpu.make_async_copy(source, target, sems.at[n])
        for n, (source, target) in enumerate(
            ((slab_hbm, slab_ref), (anchor_hbm, anchor_ref), (coef_hbm, coef_ref))
        )
    ]
    for copy in small:
        copy.start()
    large = pltpu.make_async_copy(proj_hbm, proj_ref, sems.at[3])
    large.start()
    for copy in small:
        copy.wait()

    slab = slab_ref[...].astype(F32)
    box = iota((1, BOX), 1).astype(F32)
    key = slab * BOX + box
    key = jnp.concatenate([key, key], 1)
    column = jnp.broadcast_to(key, (128, 128)).T[0:BOX]
    rank = jnp.sum(jnp.where(column < key, 1.0, 0.0), axis=0, keepdims=True)
    column = jnp.broadcast_to(rank, (128, 128)).T[0:BOX]
    lane = (iota((BOX, 128), 1) & (BOX - 1)).astype(F32)
    chosen = column == lane
    order = jnp.sum(
        jnp.where(chosen, iota((BOX, 128), 0).astype(F32), 0.0), axis=0, keepdims=True
    )
    row = iota((128, 128), 0)
    hot = jnp.where((row & (BOX - 1)).astype(F32) == rank, 1.0, 0.0)
    twice = dot(hot.astype(BF16)[:, 0:BOX], coef_ref[...]).astype(BF16)
    table = jnp.concatenate(
        [anchor_ref[...].astype(F32), slab, jnp.zeros((4, BOX), F32)], 0
    ).astype(BF16)
    table = dot(table, jnp.where(chosen, 1.0, 0.0).astype(BF16))
    later = (iota((1, 128), 1) & (BOX // 2) > 0).astype(F32)
    code = table[0:1] * WINDOW + table[3:4] - later * SHIFT
    y_place = table[1:2]
    depth = table[2:3].astype(jnp.int32)
    small_ref[0:8] = jnp.concatenate([y_place, table[2:3], jnp.zeros((6, 128), F32)], 0)
    small_ref[8:] = jnp.where(row < BOX, hot, 0.0)
    notes = pltpu.make_async_copy(small_ref, small_hbm, sems.at[8])
    notes.start()
    phases(depth, phase_ref, 4)

    large.wait()
    every = dot(proj_ref[...], twice, NT)
    total = jnp.zeros((STENCIL, 128), F32)
    for n in range(BOX):
        part = every[n * STENCIL : (n + 1) * STENCIL]
        total = jnp.where(order == float(n), part, total)
    value_ref[...] = total

    turn = y_place.astype(jnp.int32) & 3
    row = iota((16, 128), 0) & 3
    parts = []
    for k in range(4):
        value = value_ref[pl.ds(k, 16, stride=4), :]
        out = value
        for m in range(1, 4):
            moved = jnp.where(row >= m, pltpu.roll(value, m, 0), pltpu.roll(value, m + 12, 0))
            out = jnp.where(turn == m, moved, out)
        parts.append(out)
    places = jnp.where(iota((8, 128), 1) < BOX, code, y_place)[0 : ROWS - 16]
    size = SLABS // 4
    copies = []
    for wave in range(SLABS):
        total = phase_ref[wave : wave + 1, :] * parts[0]
        for k in range(1, 4):
            row = k * SLABS + wave
            total = total + phase_ref[row : row + 1, :] * parts[k]
        total = jnp.concatenate([total, places], 0).reshape(ROWS // 2, 2, 128)
        send_ref[wave] = total.astype(BF16)
        if wave % size == size - 1:
            n = wave // size
            copies.append(
                pltpu.make_async_copy(
                    send_ref.at[n * size : (n + 1) * size],
                    send_hbm.at[n * size : (n + 1) * size],
                    sems.at[4 + n],
                )
            )
            copies[-1].start()
    for copy in copies:
        copy.wait()
    notes.wait()


def spread_kernel(place_ref, recv_ref, table_ref, send_ref, pos_ref, row_ref, hot_ref):
    cells = iota((TILE, 128), 0).astype(F32)
    y_cells = iota((CY, 128), 0).astype(F32)
    upper = iota((8, 128), 0) < 4

    groups = []
    for step in range(SLABS // 4):
        tiles = []
        for n in range(4):
            tile = recv_ref[step * 4 + n].astype(F32).reshape(ROWS, 128)
            tiles.append(jnp.concatenate([tile, jnp.zeros((24 - ROWS, 128), F32)], 0))
        tiles = regroup(tiles)
        groups.append(((tiles[0], tiles[2]), (tiles[1], tiles[3])))
        places = [tile[16:17] for pair in groups[-1] for tile in pair]
        pos_ref[step] = jnp.concatenate(places + [jnp.zeros((4, 128), F32)], 0)

    def fill(step, half):
        real, imag = groups[step][half]
        code, y_place = real[16:17], imag[16:17]
        start = half * (BOXES // 2) + step * 128
        away = y_cells - y_place
        inside = jnp.where((away >= 0.0) & (away < 4.0), 1.0, 0.0).astype(BF16)
        inside = inside.reshape(8, 16, 128)
        for i in range(4):
            for c, source in enumerate((real, imag)):
                block = source[8 * (i // 2) : 8 * (i // 2) + 8]
                moved = pltpu.roll(block, 4, 0)
                pair = (block, moved) if i % 2 == 0 else (moved, block)
                both = jnp.where(upper, pair[0], pair[1])
                both = jnp.concatenate([both, both], 0).astype(BF16)
                rows = (inside * both[None]).reshape(CY, 128)
                row_ref[(2 * i + c) * CY : (2 * i + c + 1) * CY, start : start + 128] = rows
        hot_ref[:, start : start + 128] = jnp.where(cells == code, 1.0, 0.0).astype(BF16)

    count = 4
    steps = SLABS // 4 // count
    size = BOXES // 2 // count
    parts = [[None] * 4 for _ in range(2)]
    for run in range(count):
        for half in range(2):
            for step in range(run * steps, (run + 1) * steps):
                fill(step, half)
            start = half * (BOXES // 2) + run * size
            lanes = slice(start, start + size)
            for i in range(4):
                part = dot(row_ref[2 * CY * i : 2 * CY * (i + 1), lanes], hot_ref[:, lanes], NT)
                parts[half][i] = part if run == 0 else parts[half][i] + part
    planes = []
    for half in range(2):
        plane = None
        for i in range(4):
            part = jnp.concatenate([parts[half][i], jnp.zeros((2 * CY, SPAN - TILE), F32)], 1)
            plane = part if i == 0 else plane + pltpu.roll(part, WINDOW * i, 1)
        planes.append(plane)
    wave = dot(table_ref[...], jnp.concatenate(planes, 1).astype(BF16), NT)
    ac, bc = wave[:NX, :CY], wave[:NX, CY:]
    as_, bs = wave[NX:, :CY], wave[NX:, CY:]

    def put(real, imag):
        real = real.astype(BF16)
        imag = imag.astype(BF16)
        for r in range(PENCILS):
            send_ref[r, 0:LINES, :] = real[r * LINES : (r + 1) * LINES]
            send_ref[r, LINES : 2 * LINES, :] = imag[r * LINES : (r + 1) * LINES]

    @pl.when(place_ref[0] > 0)
    def _():
        put(ac + bs, bc - as_)

    @pl.when(place_ref[0] == 0)
    def _():
        line = iota((NX, CY), 0)
        real = jnp.where(line <= NX // 2, ac, bc)
        imag = jnp.where(line < NX // 2, -as_, -bs)
        put(real, jnp.where((line == 0) | (line == NX // 2), bc, imag))


def quarter(a, b, c, d, sign):
    def add(p, q):
        return (p[0] + q[0], p[1] + q[1])

    def sub(p, q):
        return (p[0] - q[0], p[1] - q[1])

    first, second, third, fourth = add(a, c), sub(a, c), add(b, d), sub(b, d)
    fourth = (-fourth[1], fourth[0]) if sign > 0 else (fourth[1], -fourth[0])
    return [add(first, third), add(second, fourth), sub(first, third), sub(second, fourth)]


def eighth(parts, sign):
    even = quarter(parts[0], parts[2], parts[4], parts[6], sign)
    odd = quarter(parts[1], parts[3], parts[5], parts[7], sign)
    root = math.sqrt(0.5)
    a, b = odd[1]
    odd[1] = ((a - sign * b) * root, (b + sign * a) * root)
    a, b = odd[2]
    odd[2] = (-sign * b, sign * a)
    a, b = odd[3]
    odd[3] = ((-a - sign * b) * root, (sign * a - b) * root)
    return [(e[0] + o[0], e[1] + o[1]) for e, o in zip(even, odd)] + [
        (e[0] - o[0], e[1] - o[1]) for e, o in zip(even, odd)
    ]


def times(value, table):
    high, low = split(value)
    return dot(high, table[0]) + dot(low, table[0]) + dot(high, table[1])


def line_kernel(place_ref, recv_ref, spec_ref, turn_ref, forward_ref, inverse_ref, send_ref):
    special = place_ref[1]
    top = (iota((8, CY), 0) == 0) & (special > 0)
    parts = []
    for q in range(PENCILS):
        real = recv_ref[q, 0:LINES, :].astype(F32)
        imag = recv_ref[q, LINES : 2 * LINES, :].astype(F32)
        first = imag[0:8]
        real = jnp.concatenate([real, jnp.where(top, first, 0.0)], 0)
        imag = jnp.concatenate(
            [jnp.where(top, 0.0, first), imag[8:], jnp.zeros((8, CY), F32)], 0
        )
        parts.append((real, imag))
    parts = eighth(parts, -1)
    lines = []
    for k in range(PENCILS):
        real, imag = parts[k]
        if k > 0:
            c = turn_ref[k : k + 1, :]
            s = turn_ref[PENCILS + k : PENCILS + k + 1, :]
            real, imag = real * c + imag * s, imag * c - real * s
        lines.append(jnp.concatenate([real, imag], 1))
    wave = times(jnp.concatenate(lines, 0), (forward_ref[0], forward_ref[1]))
    spec = spec_ref[...]
    wave = wave * jnp.concatenate([spec, spec], 1)
    wave = times(wave, (inverse_ref[0], inverse_ref[1]))
    parts = []
    for k in range(PENCILS):
        real = wave[k * MORE : (k + 1) * MORE, :CY]
        imag = wave[k * MORE : (k + 1) * MORE, CY:]
        if k > 0:
            c = turn_ref[k : k + 1, :]
            s = turn_ref[PENCILS + k : PENCILS + k + 1, :]
            real, imag = real * c - imag * s, imag * c + real * s
        parts.append((real, imag))
    parts = eighth(parts, 1)
    for q in range(PENCILS):
        real, imag = parts[q]
        send_ref[q] = jnp.concatenate(
            [
                real[0:8] - imag[LINES:],
                real[8:LINES],
                imag[0:8] + real[LINES:],
                imag[8:LINES],
            ],
            0,
        ).astype(BF16)


def sample_kernel(place_ref, pos_ref, recv_ref, table_ref, send_hbm, left_ref, wave_ref, send_ref, sems):
    real = jnp.concatenate([recv_ref[r, 0:LINES, :] for r in range(PENCILS)], 0)
    imag = jnp.concatenate([recv_ref[r, LINES : 2 * LINES, :] for r in range(PENCILS)], 0)
    real = real.astype(F32).T
    imag = imag.astype(F32).T

    def put(first, second, third, fourth):
        wave_ref[0:CY, 0:NX] = first.astype(BF16)
        wave_ref[0:CY, NX:] = second.astype(BF16)
        wave_ref[CY:, 0:NX] = third.astype(BF16)
        wave_ref[CY:, NX:] = fourth.astype(BF16)

    @pl.when(place_ref[0] > 0)
    def _():
        put(real, -imag, imag, real)

    @pl.when(place_ref[0] == 0)
    def _():
        line = iota((CY, NX), 1)
        ends = (line == 0) | (line == NX // 2)
        low = line < NX // 2
        put(
            jnp.where(ends, real, jnp.where(low, 2.0 * real, 0.0)),
            jnp.where(ends, 0.0, jnp.where(low, -2.0 * imag, 0.0)),
            jnp.where(ends, imag, jnp.where(low, 0.0, 2.0 * real)),
            jnp.where(ends, 0.0, jnp.where(low, 0.0, -2.0 * imag)),
        )

    plane = dot(wave_ref[...], table_ref[...])
    for half in range(2):
        part = plane[:, half * SPAN : (half + 1) * SPAN]
        for i in range(4):
            moved = part if i == 0 else pltpu.roll(part, SPAN - WINDOW * i, 1)
            left_ref[half, 2 * CY * i : 2 * CY * (i + 1), :] = moved[:, :TILE].astype(BF16)

    cells = iota((TILE, 128), 0).astype(F32)
    y_cells = (iota((16, 8, 128), 0) * 8 + iota((16, 8, 128), 1)).astype(F32)
    upper = iota((8, 128), 0) < 4

    def gather(step):
        quads = [step * 2, step * 2 + 1]
        found = {}
        for half in range(2):
            hot, inside = [], []
            for quad in quads:
                place = pos_ref[quad]
                code, y_place = place[2 * half : 2 * half + 1], place[2 * half + 1 : 2 * half + 2]
                hot.append(jnp.where(cells == code, 1.0, 0.0).astype(BF16))
                away = y_cells - y_place[None]
                inside.append((away >= 0.0) & (away < 4.0))
            hot = jnp.concatenate(hot, 1)
            for i in range(4):
                part = dot(left_ref[half, 2 * CY * i : 2 * CY * (i + 1), :], hot)
                for near in range(2):
                    for c in range(2):
                        block = part[c * CY : (c + 1) * CY, near * 128 : (near + 1) * 128]
                        block = jnp.where(inside[near], block.reshape(16, 8, 128), 0.0)
                        block = jnp.sum(block, axis=0)
                        found[near, c, half, i] = block + pltpu.roll(block, 4, 0)
        for near in range(2):
            tiles = []
            for c in range(2):
                for half in range(2):
                    f = [found[near, c, half, i] for i in range(4)]
                    tiles.append(
                        jnp.concatenate(
                            [jnp.where(upper, f[0], f[1]), jnp.where(upper, f[2], f[3])], 0
                        )
                    )
            for n, tile in enumerate(ungroup(tiles)):
                send_ref[quads[near] * 4 + n] = tile.astype(BF16)

    copies = []
    for step in range(SLABS // 8):
        gather(step)
        rows = slice(step * 8, (step + 1) * 8)
        copies.append(pltpu.make_async_copy(send_ref.at[rows], send_hbm.at[rows], sems.at[step]))
        copies[-1].start()
    for copy in copies:
        copy.wait()


def finish_kernel(side_ref, recv_ref, proj_ref, out_ref, value_ref, wide_ref):
    totals = [jnp.zeros((16, 128), F32) for _ in range(4)]
    for wave in range(SLABS):
        value = recv_ref[wave].astype(F32)
        terms = [side_ref[k * SLABS + wave : k * SLABS + wave + 1, :] * value for k in range(2)]
        if wave == 0:
            twice = jnp.where(iota((16, 128), 1) < BOX, 2.0, -2.0)
        else:
            twice = 2.0 * math.cos(2.0 * math.pi * wave / NZ)
        for k in range(2, 4):
            terms.append(twice * terms[k - 1] - terms[k - 2])
        totals = [total + term for total, term in zip(totals, terms)]
    turn = side_ref[NOTES : NOTES + 1, :].astype(jnp.int32) & 3
    row = iota((16, 128), 0) & 3
    for k in range(4):
        value = totals[k] + pltpu.roll(totals[k], BOX, 1)
        out = value
        for m in range(1, 4):
            moved = jnp.where(
                row + m < 4, pltpu.roll(value, 16 - m, 0), pltpu.roll(value, 4 - m, 0)
            )
            out = jnp.where(turn == m, moved, out)
        value_ref[pl.ds(k, 16, stride=4), :] = out
    back = jnp.concatenate([side_ref[ORDER:CLOSE], jnp.zeros((BOX, 128), F32)], 0).astype(BF16)
    value = dot(value_ref[...].astype(BF16), back)
    value = jnp.concatenate([value, value], 0).T[0:BOX]
    box = iota((BOX, 128), 0)
    half = (iota((BOX, 128), 1) >= STENCIL).astype(jnp.int32)
    for m in range(BOX // 2):
        wide_ref[:, 128 * m : 128 * (m + 1)] = jnp.where(
            box == 2 * m + half, value, 0.0
        ).astype(BF16)
    out_ref[...] = dot(wide_ref[...], proj_ref[...]) + side_ref[CLOSE:]


def near_kernel(ids_ref, small_ref, group_ref, near_ref, side_ref):
    phases(small_ref[1:2, :].astype(jnp.int32), side_ref, 2)
    side_ref[NOTES:CLOSE] = small_ref[0 : 8 + BOX]
    hot = jnp.where(iota((BOX, GROUP), 1) == ids_ref[...], 1.0, 0.0).astype(BF16)
    partner = dot(hot, group_ref[...]).astype(BF16)
    twice = jnp.concatenate([partner, partner], 0)
    lane = iota((FUNCS, 128), 1) & (BOX - 1)

    def step(index, total):
        start = pl.multiple_of(index * 512, 512)
        part = dot(near_ref[pl.ds(start, 512), :], twice, NT)
        for t in range(4):
            total = jnp.where(lane == index * 4 + t, part[t * FUNCS : (t + 1) * FUNCS], total)
        return total

    total = lax.fori_loop(0, BOX // 4, step, jnp.zeros((FUNCS, 128), F32))
    side_ref[CLOSE:] = total.T[0:BOX]


VMEM = pl.BlockSpec(memory_space=pltpu.VMEM)
SMEM = pl.BlockSpec(memory_space=pltpu.SMEM)
HBM = pl.BlockSpec(memory_space=pltpu.HBM)


def call(kernel, shapes, specs, scratch=(), outs=None, limit=32, flops=0, moved=0):
    return pl.pallas_call(
        kernel,
        out_shape=shapes,
        in_specs=specs,
        out_specs=outs or jax.tree.map(lambda _: VMEM, shapes),
        scratch_shapes=list(scratch),
        compiler_params=pltpu.CompilerParams(vmem_limit_bytes=limit * 1024 * 1024),
        cost_estimate=pl.CostEstimate(flops=flops, bytes_accessed=moved, transcendentals=0),
    )


def resident(*arrays, space=pltpu.HBM):
    return [pltpu.with_memory_space_constraint(a, space) for a in arrays]


def struct(*shape, kind=F32):
    return jax.ShapeDtypeStruct(shape, kind)


def project(anchors, slabs, coefficients, flat):
    return call(
        project_kernel,
        (
            pltpu.HBM((SLABS, ROWS // 2, 2, 128), BF16),
            pltpu.HBM((SMALL, 128), F32),
        ),
        [HBM] * 4,
        [
            pltpu.VMEM((SLABS, ROWS // 2, 2, 128), BF16),
            pltpu.VMEM((SMALL, 128), F32),
            pltpu.VMEM((4 * SLABS, 128), F32),
            pltpu.VMEM((STENCIL, 128), F32),
            pltpu.VMEM(anchors.shape, jnp.int32),
            pltpu.VMEM(slabs.shape, jnp.int32),
            pltpu.VMEM(coefficients.shape, BF16),
            pltpu.VMEM(flat.shape, BF16),
            pltpu.SemaphoreType.DMA((9,)),
        ],
        outs=(HBM, HBM),
        limit=8,
        flops=2 * BOXES * FUNCS * 128,
        moved=2 << 20,
    )(*resident(anchors, slabs, coefficients, flat))


def spread(place, received, table):
    return call(
        spread_kernel,
        (struct(PENCILS, 2 * LINES, CY, kind=BF16), struct(SLABS // 4, 8, 128)),
        [SMEM] + [VMEM] * 2,
        [pltpu.VMEM((8 * CY, BOXES), BF16), pltpu.VMEM((TILE, BOXES), BF16)],
        limit=28,
        flops=2 * BOXES * TILE * 8 * CY,
        moved=4 << 20,
    )(place, received, table)


def lines(place, received, spec, turn, forward, inverse):
    return call(
        line_kernel,
        struct(PENCILS, 2 * LINES, CY, kind=BF16),
        [SMEM] + [VMEM] * 5,
        limit=12,
        flops=2 * 6 * PENCILS * MORE * 256 * 256,
        moved=2 << 20,
    )(place, received, spec, turn, forward, inverse)


def sample(place, pos, received, table):
    return call(
        sample_kernel,
        pltpu.HBM((SLABS, 16, 128), BF16),
        [SMEM] + [VMEM] * 3,
        [
            pltpu.VMEM((2, 8 * CY, TILE), BF16),
            pltpu.VMEM((2 * CY, 2 * NX), BF16),
            pltpu.VMEM((SLABS, 16, 128), BF16),
            pltpu.SemaphoreType.DMA((SLABS // 8,)),
        ],
        outs=HBM,
        limit=16,
        flops=2 * BOXES * TILE * 8 * CY,
        moved=4 << 20,
    )(place, pos, received, table)


def finish(side, received, flat):
    return call(
        finish_kernel,
        struct(BOX, FUNCS),
        [VMEM] * 3,
        [pltpu.VMEM((STENCIL, 128), F32), pltpu.VMEM((BOX, BOX * STENCIL), BF16)],
        limit=8,
        flops=2 * BOX * BOXES * FUNCS,
        moved=2 << 20,
    )(*resident(side, space=pltpu.VMEM), received, flat)


def near(ids, small, group, blocks):
    return call(
        near_kernel,
        pltpu.VMEM((SIDE, 128), F32),
        [VMEM] * 4,
        limit=8,
        flops=2 * BOX * FUNCS * FUNCS * 128,
        moved=3 << 20,
    )(ids, small, group, blocks)


def arrange(spectrum, slab, pencil):
    first, second = spectrum[:, 0, :], spectrum[:, 1, :]
    chosen = jnp.where((slab == 0) & (pencil >= PENCILS // 2), second, first)
    head = jnp.where((slab == 0) & (pencil == PENCILS // 2), first[0:1], chosen[0:1])
    rows = jnp.concatenate([head, chosen[1:], jnp.broadcast_to(second[0:1], (8, NY))], 0)
    rows = rows * jnp.where(slab == 0, 1.0, 2.0) * (1.0 / (NX * NY * NZ))
    return rows.reshape(MORE, CY, PENCILS).transpose(2, 0, 1).reshape(PENCILS * MORE, CY)


def per_device(coefficients, projection, near_blocks, near_ids, grid_slab, anchors, spectrum):
    slab = lax.axis_index("slab")
    pencil = lax.axis_index("pencil")
    special = (slab == 0) & (pencil % (PENCILS // 2) == 0)
    place = jnp.stack([slab, special.astype(jnp.int32)]).astype(jnp.int32)
    flat = projection.reshape(BOX * STENCIL, FUNCS)
    table = jnp.asarray(x_table().astype(BF16))
    forward, inverse, turn = y_tables()
    forward, inverse = np.stack(halves(forward)), np.stack(halves(inverse))

    send, small = project(anchors, grid_slab.reshape(1, BOX), coefficients, flat)
    received = lax.all_to_all(send, "slab", split_axis=0, concat_axis=0, tiled=True)
    spec = arrange(spectrum, slab, pencil)
    received, spec, place = lax.optimization_barrier((received, spec, place))
    send, pos = spread(place, received, table)
    received = lax.all_to_all(send, "pencil", split_axis=0, concat_axis=0, tiled=True)
    send = lines(place, received, spec, turn, forward, inverse)
    received = lax.all_to_all(send, "pencil", split_axis=0, concat_axis=0, tiled=True)
    send = sample(place, pos, received, table)
    send, own = lax.optimization_barrier((send, coefficients))
    received = lax.all_to_all(send, "slab", split_axis=0, concat_axis=0, tiled=True)
    group = lax.all_gather(own, "pencil", axis=0, tiled=True)
    blocks = near_blocks.reshape(BOX * FUNCS, FUNCS)
    side = near(near_ids & (GROUP - 1), small, group, blocks)
    return finish(side, received, flat)


def solution(mesh):
    placed = (
        P(("slab", "pencil"), None),
        P(("slab", "pencil"), None, None),
        P(("slab", "pencil"), None, None, None),
        P(("slab", "pencil"), None),
        P(("slab", "pencil"), None),
        P(None, ("slab", "pencil")),
        P("pencil", "slab", None),
    )
    return jax.shard_map(
        per_device,
        mesh=mesh,
        in_specs=placed,
        out_specs=P(("slab", "pencil"), None),
        check_vma=False,
    )
```

```python
import math

import jax
import jax.numpy as jnp
import numpy as np
from jax import lax
from jax.experimental import pallas as pl
from jax.experimental.pallas import tpu as pltpu
from jax.sharding import PartitionSpec as P

SLABS = 64
PENCILS = 8
BOX = 64
FUNCS = 128
STENCIL = 64
CX = 8
CY = 128
NX = 512
NY = 1024
NZ = 128
GROUP = BOX * PENCILS
ROWS = 18
LINES = NX // PENCILS
MORE = LINES + 8
BOXES = SLABS * BOX
SMALL = 8 + 128
NOTES = 2 * SLABS
ORDER = NOTES + 8
CLOSE = ORDER + BOX
SIDE = CLOSE + BOX
TILE = 256
WINDOW = 48
SHIFT = SLABS - WINDOW
SPAN = CX * WINDOW

F32 = jnp.float32
BF16 = jnp.bfloat16
NT = (((1,), (1,)), ((), ()))
NN = (((1,), (0,)), ((), ()))


def halves(table):
    table = np.asarray(table, np.float32)
    high = table.astype(BF16)
    low = (table - high.astype(np.float32)).astype(BF16)
    return high, low


def x_table():
    half, offset, slab = np.meshgrid(
        np.arange(2), np.arange(CX), np.arange(WINDOW), indexing="ij"
    )
    cells = (CX * (slab + SHIFT * half) + offset).reshape(-1)
    phase = np.outer(np.arange(NX), cells) % NX * (2.0 * math.pi / NX)
    return np.concatenate([np.cos(phase), np.sin(phase)], 0)


def y_tables():
    phase = np.outer(np.arange(CY), np.arange(CY)) % CY * (2.0 * math.pi / CY)
    c, s = np.cos(phase), np.sin(phase)
    forward = np.block([[c, -s], [s, c]])
    inverse = np.block([[c, s], [-s, c]])
    turn = np.outer(np.arange(PENCILS), np.arange(CY)) * (2.0 * math.pi / NY)
    turn = np.concatenate([np.cos(turn), np.sin(turn)], 0).astype(np.float32)
    return forward, inverse, turn


def cosine_coefficients():
    fit = np.polynomial.chebyshev.Chebyshev.interpolate(
        lambda w: np.cos(2.0 * math.pi * np.sqrt(w)), 9, domain=[0.0, 0.25]
    )
    return [float(v) for v in fit.convert(kind=np.polynomial.Polynomial).coef]


COSINE = cosine_coefficients()


def cosine_of(step):
    u = (step.astype(F32) - (NZ // 2)) * (1.0 / NZ)
    w = u * u
    total = jnp.full_like(w, COSINE[-1])
    for value in COSINE[-2::-1]:
        total = total * w + value
    return -total


def iota(shape, axis):
    return lax.broadcasted_iota(jnp.int32, shape, axis)


def dot(a, b, dims=NN):
    return lax.dot_general(a, b, dims, preferred_element_type=F32)


def one_hot(cells, code):
    return jnp.where(cells == code.astype(BF16), jnp.ones((), BF16), jnp.zeros((), BF16))


def split(value):
    high = value.astype(BF16)
    return high, (value - high.astype(F32)).astype(BF16)


def swap(first, other, width):
    even = iota(first.shape, 1) & width == 0
    return (
        jnp.where(even, first, pltpu.roll(other, width, 1)),
        jnp.where(even, pltpu.roll(first, 128 - width, 1), other),
    )


def regroup(tiles):
    a, c = swap(tiles[0], tiles[2], 64)
    b, d = swap(tiles[1], tiles[3], 64)
    return swap(a, b, 32) + swap(c, d, 32)


def ungroup(tiles):
    a, b = swap(tiles[0], tiles[1], 32)
    c, d = swap(tiles[2], tiles[3], 32)
    first, third = swap(a, c, 64)
    second, fourth = swap(b, d, 64)
    return first, second, third, fourth


def phases(depth, phase_ref, count):
    second = (iota((SLABS, 128), 1) >= BOX).astype(jnp.int32)
    wave = iota((SLABS, 128), 0)
    for k in range(count):
        z = depth + k
        step = jnp.where(wave == 0, second * (NZ // 2) * z, wave * z + second * (NZ // 4))
        phase_ref[k * SLABS : (k + 1) * SLABS] = cosine_of(step & (NZ - 1))


def project_kernel(
    anchor_hbm, slab_hbm, coef_hbm, proj_hbm,
    send_hbm, small_hbm,
    send_ref, small_ref, phase_ref, value_ref, anchor_ref, slab_ref, coef_ref, proj_ref, sems,
):
    small = [
        pltpu.make_async_copy(source, target, sems.at[n])
        for n, (source, target) in enumerate(
            ((slab_hbm, slab_ref), (anchor_hbm, anchor_ref), (coef_hbm, coef_ref))
        )
    ]
    for copy in small:
        copy.start()
    large = pltpu.make_async_copy(proj_hbm, proj_ref, sems.at[3])
    large.start()
    for copy in small:
        copy.wait()

    slab = slab_ref[...].astype(F32)
    box = iota((1, BOX), 1).astype(F32)
    key = slab * BOX + box
    key = jnp.concatenate([key, key], 1)
    column = jnp.broadcast_to(key, (128, 128)).T[0:BOX]
    rank = jnp.sum(jnp.where(column < key, 1.0, 0.0), axis=0, keepdims=True)
    column = jnp.broadcast_to(rank, (128, 128)).T[0:BOX]
    lane = (iota((BOX, 128), 1) & (BOX - 1)).astype(F32)
    chosen = column == lane
    order = jnp.sum(
        jnp.where(chosen, iota((BOX, 128), 0).astype(F32), 0.0), axis=0, keepdims=True
    )
    row = iota((128, 128), 0)
    hot = jnp.where((row & (BOX - 1)).astype(F32) == rank, 1.0, 0.0)
    twice = dot(hot.astype(BF16)[:, 0:BOX], coef_ref[...]).astype(BF16)
    table = jnp.concatenate(
        [anchor_ref[...].astype(F32), slab, jnp.zeros((4, BOX), F32)], 0
    ).astype(BF16)
    table = dot(table, jnp.where(chosen, 1.0, 0.0).astype(BF16))
    later = (iota((1, 128), 1) & (BOX // 2) > 0).astype(F32)
    code = table[0:1] * WINDOW + table[3:4] - later * SHIFT
    y_place = table[1:2]
    depth = table[2:3].astype(jnp.int32)
    small_ref[0:8] = jnp.concatenate([y_place, table[2:3], jnp.zeros((6, 128), F32)], 0)
    small_ref[8:] = jnp.where(row < BOX, hot, 0.0)
    notes = pltpu.make_async_copy(small_ref, small_hbm, sems.at[8])
    notes.start()
    phases(depth, phase_ref, 4)

    large.wait()
    every = dot(proj_ref[...], twice, NT)
    total = jnp.zeros((STENCIL, 128), F32)
    for n in range(BOX):
        part = every[n * STENCIL : (n + 1) * STENCIL]
        total = jnp.where(order == float(n), part, total)
    value_ref[...] = total

    turn = y_place.astype(jnp.int32) & 3
    row = iota((16, 128), 0) & 3
    parts = []
    for k in range(4):
        value = value_ref[pl.ds(k, 16, stride=4), :]
        out = value
        for m in range(1, 4):
            moved = jnp.where(row >= m, pltpu.roll(value, m, 0), pltpu.roll(value, m + 12, 0))
            out = jnp.where(turn == m, moved, out)
        parts.append(out)
    places = jnp.where(iota((8, 128), 1) < BOX, code, y_place)[0 : ROWS - 16]
    size = SLABS // 4
    copies = []
    for wave in range(SLABS):
        total = phase_ref[wave : wave + 1, :] * parts[0]
        for k in range(1, 4):
            row = k * SLABS + wave
            total = total + phase_ref[row : row + 1, :] * parts[k]
        total = jnp.concatenate([total, places], 0).reshape(ROWS // 2, 2, 128)
        send_ref[wave] = total.astype(BF16)
        if wave % size == size - 1:
            n = wave // size
            copies.append(
                pltpu.make_async_copy(
                    send_ref.at[n * size : (n + 1) * size],
                    send_hbm.at[n * size : (n + 1) * size],
                    sems.at[4 + n],
                )
            )
            copies[-1].start()
    for copy in copies:
        copy.wait()
    notes.wait()


def spread_kernel(place_ref, recv_ref, table_ref, send_ref, pos_ref, row_ref, hot_ref):
    cells = iota((TILE, 128), 0).astype(F32).astype(BF16)
    y_cells = iota((CY, 128), 0).astype(F32)
    upper = iota((8, 128), 0) < 4

    groups = []
    for step in range(SLABS // 4):
        tiles = []
        for n in range(4):
            tile = recv_ref[step * 4 + n].astype(F32).reshape(ROWS, 128)
            tiles.append(jnp.concatenate([tile, jnp.zeros((24 - ROWS, 128), F32)], 0))
        tiles = regroup(tiles)
        groups.append(((tiles[0], tiles[2]), (tiles[1], tiles[3])))
        places = [tile[16:17] for pair in groups[-1] for tile in pair]
        pos_ref[step] = jnp.concatenate(places + [jnp.zeros((4, 128), F32)], 0)

    def fill(step, half):
        real, imag = groups[step][half]
        code, y_place = real[16:17], imag[16:17]
        start = half * (BOXES // 2) + step * 128
        away = y_cells - y_place
        inside = jnp.clip(2.5 - jnp.abs(away.astype(BF16) - 1.5), 0.0, 1.0)
        inside = inside.reshape(8, 16, 128)
        for i in range(4):
            for c, source in enumerate((real, imag)):
                block = source[8 * (i // 2) : 8 * (i // 2) + 8]
                moved = pltpu.roll(block, 4, 0)
                pair = (block, moved) if i % 2 == 0 else (moved, block)
                both = jnp.where(upper, pair[0], pair[1])
                both = jnp.concatenate([both, both], 0).astype(BF16)
                rows = (inside * both[None]).reshape(CY, 128)
                row_ref[(2 * i + c) * CY : (2 * i + c + 1) * CY, start : start + 128] = rows
        hot_ref[:, start : start + 128] = one_hot(cells, code)

    count = 4
    steps = SLABS // 4 // count
    size = BOXES // 2 // count
    parts = [[None] * 4 for _ in range(2)]
    for run in range(count):
        for half in range(2):
            for step in range(run * steps, (run + 1) * steps):
                fill(step, half)
            start = half * (BOXES // 2) + run * size
            lanes = slice(start, start + size)
            for i in range(4):
                part = dot(row_ref[2 * CY * i : 2 * CY * (i + 1), lanes], hot_ref[:, lanes], NT)
                parts[half][i] = part if run == 0 else parts[half][i] + part
    planes = []
    for half in range(2):
        plane = None
        for i in range(4):
            part = jnp.concatenate([parts[half][i], jnp.zeros((2 * CY, SPAN - TILE), F32)], 1)
            plane = part if i == 0 else plane + pltpu.roll(part, WINDOW * i, 1)
        planes.append(plane)
    wave = dot(table_ref[...], jnp.concatenate(planes, 1).astype(BF16), NT)
    ac, bc = wave[:NX, :CY], wave[:NX, CY:]
    as_, bs = wave[NX:, :CY], wave[NX:, CY:]

    def put(real, imag):
        real = real.astype(BF16)
        imag = imag.astype(BF16)
        for r in range(PENCILS):
            send_ref[r, 0:LINES, :] = real[r * LINES : (r + 1) * LINES]
            send_ref[r, LINES : 2 * LINES, :] = imag[r * LINES : (r + 1) * LINES]

    @pl.when(place_ref[0] > 0)
    def _():
        put(ac + bs, bc - as_)

    @pl.when(place_ref[0] == 0)
    def _():
        line = iota((NX, CY), 0)
        real = jnp.where(line <= NX // 2, ac, bc)
        imag = jnp.where(line < NX // 2, -as_, -bs)
        put(real, jnp.where((line == 0) | (line == NX // 2), bc, imag))


def quarter(a, b, c, d, sign):
    def add(p, q):
        return (p[0] + q[0], p[1] + q[1])

    def sub(p, q):
        return (p[0] - q[0], p[1] - q[1])

    first, second, third, fourth = add(a, c), sub(a, c), add(b, d), sub(b, d)
    fourth = (-fourth[1], fourth[0]) if sign > 0 else (fourth[1], -fourth[0])
    return [add(first, third), add(second, fourth), sub(first, third), sub(second, fourth)]


def eighth(parts, sign):
    even = quarter(parts[0], parts[2], parts[4], parts[6], sign)
    odd = quarter(parts[1], parts[3], parts[5], parts[7], sign)
    root = math.sqrt(0.5)
    a, b = odd[1]
    odd[1] = ((a - sign * b) * root, (b + sign * a) * root)
    a, b = odd[2]
    odd[2] = (-sign * b, sign * a)
    a, b = odd[3]
    odd[3] = ((-a - sign * b) * root, (sign * a - b) * root)
    return [(e[0] + o[0], e[1] + o[1]) for e, o in zip(even, odd)] + [
        (e[0] - o[0], e[1] - o[1]) for e, o in zip(even, odd)
    ]


def times(value, table):
    high, low = split(value)
    return dot(high, table[0]) + dot(low, table[0]) + dot(high, table[1])


def line_kernel(place_ref, recv_ref, spec_ref, turn_ref, forward_ref, inverse_ref, send_ref):
    special = place_ref[1]
    top = (iota((8, CY), 0) == 0) & (special > 0)
    parts = []
    for q in range(PENCILS):
        real = recv_ref[q, 0:LINES, :].astype(F32)
        imag = recv_ref[q, LINES : 2 * LINES, :].astype(F32)
        first = imag[0:8]
        real = jnp.concatenate([real, jnp.where(top, first, 0.0)], 0)
        imag = jnp.concatenate(
            [jnp.where(top, 0.0, first), imag[8:], jnp.zeros((8, CY), F32)], 0
        )
        parts.append((real, imag))
    parts = eighth(parts, -1)
    lines = []
    for k in range(PENCILS):
        real, imag = parts[k]
        if k > 0:
            c = turn_ref[k : k + 1, :]
            s = turn_ref[PENCILS + k : PENCILS + k + 1, :]
            real, imag = real * c + imag * s, imag * c - real * s
        lines.append(jnp.concatenate([real, imag], 1))
    wave = times(jnp.concatenate(lines, 0), (forward_ref[0], forward_ref[1]))
    spec = spec_ref[...]
    wave = wave * jnp.concatenate([spec, spec], 1)
    wave = times(wave, (inverse_ref[0], inverse_ref[1]))
    parts = []
    for k in range(PENCILS):
        real = wave[k * MORE : (k + 1) * MORE, :CY]
        imag = wave[k * MORE : (k + 1) * MORE, CY:]
        if k > 0:
            c = turn_ref[k : k + 1, :]
            s = turn_ref[PENCILS + k : PENCILS + k + 1, :]
            real, imag = real * c - imag * s, imag * c + real * s
        parts.append((real, imag))
    parts = eighth(parts, 1)
    for q in range(PENCILS):
        real, imag = parts[q]
        send_ref[q] = jnp.concatenate(
            [
                real[0:8] - imag[LINES:],
                real[8:LINES],
                imag[0:8] + real[LINES:],
                imag[8:LINES],
            ],
            0,
        ).astype(BF16)


def sample_kernel(place_ref, pos_ref, recv_ref, table_ref, send_hbm, left_ref, wave_ref, send_ref, sems):
    real = jnp.concatenate([recv_ref[r, 0:LINES, :] for r in range(PENCILS)], 0)
    imag = jnp.concatenate([recv_ref[r, LINES : 2 * LINES, :] for r in range(PENCILS)], 0)
    real = real.astype(F32).T
    imag = imag.astype(F32).T

    def put(first, second, third, fourth):
        wave_ref[0:CY, 0:NX] = first.astype(BF16)
        wave_ref[0:CY, NX:] = second.astype(BF16)
        wave_ref[CY:, 0:NX] = third.astype(BF16)
        wave_ref[CY:, NX:] = fourth.astype(BF16)

    @pl.when(place_ref[0] > 0)
    def _():
        put(real, -imag, imag, real)

    @pl.when(place_ref[0] == 0)
    def _():
        line = iota((CY, NX), 1)
        ends = (line == 0) | (line == NX // 2)
        low = line < NX // 2
        put(
            jnp.where(ends, real, jnp.where(low, 2.0 * real, 0.0)),
            jnp.where(ends, 0.0, jnp.where(low, -2.0 * imag, 0.0)),
            jnp.where(ends, imag, jnp.where(low, 0.0, 2.0 * real)),
            jnp.where(ends, 0.0, jnp.where(low, 0.0, -2.0 * imag)),
        )

    plane = dot(wave_ref[...], table_ref[...])
    for half in range(2):
        part = plane[:, half * SPAN : (half + 1) * SPAN]
        for i in range(4):
            moved = part if i == 0 else pltpu.roll(part, SPAN - WINDOW * i, 1)
            left_ref[half, 2 * CY * i : 2 * CY * (i + 1), :] = moved[:, :TILE].astype(BF16)

    cells = iota((TILE, 128), 0).astype(F32).astype(BF16)
    y_cells = (iota((16, 8, 128), 0) * 8 + iota((16, 8, 128), 1)).astype(F32)
    upper = iota((8, 128), 0) < 4

    def gather(step):
        quads = [step * 2, step * 2 + 1]
        found = {}
        for half in range(2):
            hot, inside = [], []
            for quad in quads:
                place = pos_ref[quad]
                code, y_place = place[2 * half : 2 * half + 1], place[2 * half + 1 : 2 * half + 2]
                hot.append(one_hot(cells, code))
                away = y_cells - y_place[None]
                inside.append((away >= 0.0) & (away < 4.0))
            hot = jnp.concatenate(hot, 1)
            for i in range(4):
                part = dot(left_ref[half, 2 * CY * i : 2 * CY * (i + 1), :], hot)
                for near in range(2):
                    for c in range(2):
                        block = part[c * CY : (c + 1) * CY, near * 128 : (near + 1) * 128]
                        block = jnp.where(inside[near], block.reshape(16, 8, 128), 0.0)
                        block = jnp.sum(block, axis=0)
                        found[near, c, half, i] = block + pltpu.roll(block, 4, 0)
        for near in range(2):
            tiles = []
            for c in range(2):
                for half in range(2):
                    f = [found[near, c, half, i] for i in range(4)]
                    tiles.append(
                        jnp.concatenate(
                            [jnp.where(upper, f[0], f[1]), jnp.where(upper, f[2], f[3])], 0
                        )
                    )
            for n, tile in enumerate(ungroup(tiles)):
                send_ref[quads[near] * 4 + n] = tile.astype(BF16)

    copies = []
    for step in range(SLABS // 8):
        gather(step)
        rows = slice(step * 8, (step + 1) * 8)
        copies.append(pltpu.make_async_copy(send_ref.at[rows], send_hbm.at[rows], sems.at[step]))
        copies[-1].start()
    for copy in copies:
        copy.wait()


def finish_kernel(side_ref, recv_ref, proj_ref, out_ref, value_ref, wide_ref):
    totals = [jnp.zeros((16, 128), F32) for _ in range(4)]
    for wave in range(SLABS):
        value = recv_ref[wave].astype(F32)
        terms = [side_ref[k * SLABS + wave : k * SLABS + wave + 1, :] * value for k in range(2)]
        if wave == 0:
            twice = jnp.where(iota((16, 128), 1) < BOX, 2.0, -2.0)
        else:
            twice = 2.0 * math.cos(2.0 * math.pi * wave / NZ)
        for k in range(2, 4):
            terms.append(twice * terms[k - 1] - terms[k - 2])
        totals = [total + term for total, term in zip(totals, terms)]
    turn = side_ref[NOTES : NOTES + 1, :].astype(jnp.int32) & 3
    row = iota((16, 128), 0) & 3
    for k in range(4):
        value = totals[k] + pltpu.roll(totals[k], BOX, 1)
        out = value
        for m in range(1, 4):
            moved = jnp.where(
                row + m < 4, pltpu.roll(value, 16 - m, 0), pltpu.roll(value, 4 - m, 0)
            )
            out = jnp.where(turn == m, moved, out)
        value_ref[pl.ds(k, 16, stride=4), :] = out
    back = jnp.concatenate([side_ref[ORDER:CLOSE], jnp.zeros((BOX, 128), F32)], 0).astype(BF16)
    value = dot(value_ref[...].astype(BF16), back)
    value = jnp.concatenate([value, value], 0).T[0:BOX]
    box = iota((BOX, 128), 0)
    half = (iota((BOX, 128), 1) >= STENCIL).astype(jnp.int32)
    for m in range(BOX // 2):
        wide_ref[:, 128 * m : 128 * (m + 1)] = jnp.where(
            box == 2 * m + half, value, 0.0
        ).astype(BF16)
    out_ref[...] = dot(wide_ref[...], proj_ref[...]) + side_ref[CLOSE:]


def near_kernel(ids_ref, small_ref, group_ref, near_ref, side_ref):
    phases(small_ref[1:2, :].astype(jnp.int32), side_ref, 2)
    side_ref[NOTES:CLOSE] = small_ref[0 : 8 + BOX]
    hot = jnp.where(iota((BOX, GROUP), 1) == ids_ref[...], 1.0, 0.0).astype(BF16)
    partner = dot(hot, group_ref[...]).astype(BF16)
    twice = jnp.concatenate([partner, partner], 0)
    lane = iota((FUNCS, 128), 1) & (BOX - 1)

    def step(index, total):
        start = pl.multiple_of(index * 512, 512)
        part = dot(near_ref[pl.ds(start, 512), :], twice, NT)
        for t in range(4):
            total = jnp.where(lane == index * 4 + t, part[t * FUNCS : (t + 1) * FUNCS], total)
        return total

    total = lax.fori_loop(0, BOX // 4, step, jnp.zeros((FUNCS, 128), F32))
    side_ref[CLOSE:] = total.T[0:BOX]


VMEM = pl.BlockSpec(memory_space=pltpu.VMEM)
SMEM = pl.BlockSpec(memory_space=pltpu.SMEM)
HBM = pl.BlockSpec(memory_space=pltpu.HBM)


def call(kernel, shapes, specs, scratch=(), outs=None, limit=32, flops=0, moved=0):
    return pl.pallas_call(
        kernel,
        out_shape=shapes,
        in_specs=specs,
        out_specs=outs or jax.tree.map(lambda _: VMEM, shapes),
        scratch_shapes=list(scratch),
        compiler_params=pltpu.CompilerParams(vmem_limit_bytes=limit * 1024 * 1024),
        cost_estimate=pl.CostEstimate(flops=flops, bytes_accessed=moved, transcendentals=0),
    )


def resident(*arrays, space=pltpu.HBM):
    return [pltpu.with_memory_space_constraint(a, space) for a in arrays]


def struct(*shape, kind=F32):
    return jax.ShapeDtypeStruct(shape, kind)


def project(anchors, slabs, coefficients, flat):
    return call(
        project_kernel,
        (
            pltpu.HBM((SLABS, ROWS // 2, 2, 128), BF16),
            pltpu.HBM((SMALL, 128), F32),
        ),
        [HBM] * 4,
        [
            pltpu.VMEM((SLABS, ROWS // 2, 2, 128), BF16),
            pltpu.VMEM((SMALL, 128), F32),
            pltpu.VMEM((4 * SLABS, 128), F32),
            pltpu.VMEM((STENCIL, 128), F32),
            pltpu.VMEM(anchors.shape, jnp.int32),
            pltpu.VMEM(slabs.shape, jnp.int32),
            pltpu.VMEM(coefficients.shape, BF16),
            pltpu.VMEM(flat.shape, BF16),
            pltpu.SemaphoreType.DMA((9,)),
        ],
        outs=(HBM, HBM),
        limit=8,
        flops=2 * BOXES * FUNCS * 128,
        moved=2 << 20,
    )(*resident(anchors, slabs, coefficients, flat))


def spread(place, received, table):
    return call(
        spread_kernel,
        (struct(PENCILS, 2 * LINES, CY, kind=BF16), struct(SLABS // 4, 8, 128)),
        [SMEM] + [VMEM] * 2,
        [pltpu.VMEM((8 * CY, BOXES), BF16), pltpu.VMEM((TILE, BOXES), BF16)],
        limit=28,
        flops=2 * BOXES * TILE * 8 * CY,
        moved=4 << 20,
    )(place, received, table)


def lines(place, received, spec, turn, forward, inverse):
    return call(
        line_kernel,
        struct(PENCILS, 2 * LINES, CY, kind=BF16),
        [SMEM] + [VMEM] * 5,
        limit=12,
        flops=2 * 6 * PENCILS * MORE * 256 * 256,
        moved=2 << 20,
    )(place, received, spec, turn, forward, inverse)


def sample(place, pos, received, table):
    return call(
        sample_kernel,
        pltpu.HBM((SLABS, 16, 128), BF16),
        [SMEM] + [VMEM] * 3,
        [
            pltpu.VMEM((2, 8 * CY, TILE), BF16),
            pltpu.VMEM((2 * CY, 2 * NX), BF16),
            pltpu.VMEM((SLABS, 16, 128), BF16),
            pltpu.SemaphoreType.DMA((SLABS // 8,)),
        ],
        outs=HBM,
        limit=16,
        flops=2 * BOXES * TILE * 8 * CY,
        moved=4 << 20,
    )(place, pos, received, table)


def finish(side, received, flat):
    return call(
        finish_kernel,
        struct(BOX, FUNCS),
        [VMEM] * 3,
        [pltpu.VMEM((STENCIL, 128), F32), pltpu.VMEM((BOX, BOX * STENCIL), BF16)],
        limit=8,
        flops=2 * BOX * BOXES * FUNCS,
        moved=2 << 20,
    )(*resident(side, space=pltpu.VMEM), received, flat)


def near(ids, small, group, blocks):
    return call(
        near_kernel,
        pltpu.VMEM((SIDE, 128), F32),
        [VMEM] * 4,
        limit=8,
        flops=2 * BOX * FUNCS * FUNCS * 128,
        moved=3 << 20,
    )(ids, small, group, blocks)


def arrange(spectrum, slab, pencil):
    first, second = spectrum[:, 0, :], spectrum[:, 1, :]
    chosen = jnp.where((slab == 0) & (pencil >= PENCILS // 2), second, first)
    head = jnp.where((slab == 0) & (pencil == PENCILS // 2), first[0:1], chosen[0:1])
    rows = jnp.concatenate([head, chosen[1:], jnp.broadcast_to(second[0:1], (8, NY))], 0)
    rows = rows * jnp.where(slab == 0, 1.0, 2.0) * (1.0 / (NX * NY * NZ))
    return rows.reshape(MORE, CY, PENCILS).transpose(2, 0, 1).reshape(PENCILS * MORE, CY)


def per_device(coefficients, projection, near_blocks, near_ids, grid_slab, anchors, spectrum):
    slab = lax.axis_index("slab")
    pencil = lax.axis_index("pencil")
    special = (slab == 0) & (pencil % (PENCILS // 2) == 0)
    place = jnp.stack([slab, special.astype(jnp.int32)]).astype(jnp.int32)
    flat = projection.reshape(BOX * STENCIL, FUNCS)
    table = jnp.asarray(x_table().astype(BF16))
    forward, inverse, turn = y_tables()
    forward, inverse = np.stack(halves(forward)), np.stack(halves(inverse))

    send, small = project(anchors, grid_slab.reshape(1, BOX), coefficients, flat)
    received = lax.all_to_all(send, "slab", split_axis=0, concat_axis=0, tiled=True)
    spec = arrange(spectrum, slab, pencil)
    received, spec, place = lax.optimization_barrier((received, spec, place))
    send, pos = spread(place, received, table)
    received = lax.all_to_all(send, "pencil", split_axis=0, concat_axis=0, tiled=True)
    send = lines(place, received, spec, turn, forward, inverse)
    received = lax.all_to_all(send, "pencil", split_axis=0, concat_axis=0, tiled=True)
    send = sample(place, pos, received, table)
    send, own = lax.optimization_barrier((send, coefficients))
    received = lax.all_to_all(send, "slab", split_axis=0, concat_axis=0, tiled=True)
    group = lax.all_gather(own, "pencil", axis=0, tiled=True)
    blocks = near_blocks.reshape(BOX * FUNCS, FUNCS)
    side = near(near_ids & (GROUP - 1), small, group, blocks)
    return finish(side, received, flat)


def solution(mesh):
    placed = (
        P(("slab", "pencil"), None),
        P(("slab", "pencil"), None, None),
        P(("slab", "pencil"), None, None, None),
        P(("slab", "pencil"), None),
        P(("slab", "pencil"), None),
        P(None, ("slab", "pencil")),
        P("pencil", "slab", None),
    )
    return jax.shard_map(
        per_device,
        mesh=mesh,
        in_specs=placed,
        out_specs=P(("slab", "pencil"), None),
        check_vma=False,
    )
```
